256 devices in a mesh: row: 32 (over z, y), col: 8 (over x, core).
Axes of the slice: x: 4, y: 4, z: 8, core: 2. Of those that a mesh axis runs over, the one named last changes fastest.
Arguments:
- activations: bfloat16 [2048, 8192], P('col', 'row'), may hold values from -640 to 640
- output_grads: bfloat16 [2048, 24576], P('row', 'col'), may hold values from -640 to 640
- first_codes: int32 [8192, 12288], P('row', 'col'), may hold values from 0 to 255
- second_codes: int32 [8192, 12288], P('row', 'col'), may hold values from 0 to 255
- first_scales: float32 [8192, 192], P('row', 'col'), may hold values from 0.1 to 1
- second_rows: float32 [8192], P('row'), may hold values from 0.03 to 0.3
- second_cols: float32 [24576], P('col'), may hold values from 0.03 to 0.3
Outputs:
- update: float32 [8192, 24576], P('row', 'col')
- first_normed: bfloat16 [8192, 24576], P('row', 'col')
- first_peaks: float32 [8192, 192], P('row', 'col')
- second_normed: bfloat16 [8192, 24576], P('row', 'col')
- second_row_peaks: float32 [8192], P('row')
- second_col_peaks: float32 [24576], P('col')
The draws below stay inside these ranges and needn't reach their ends.
All inputs are finite; a program needn't handle non-finite values. Where the reference program divides by a largest or mean magnitude, that divisor is 1e-20 or more.
Results may differ from the reference program's by a relative error of at most 0.001.
Values may be sent and summed in bfloat16 or wider, within the bound.
A program may use at most 128 MiB of HBM per device.

```python
import math
import jax
import jax.numpy as jnp
from jax import lax

D = 8192
FF = 24576
TOKENS = 2048
N_ROW = 32


def token_signs(key):
    bits = jax.random.randint(key, (6, 16), 0, 2)
    signs = (2 * bits - 1).astype(jnp.float32)
    return jnp.repeat(signs, TOKENS // 16, axis=1)


def loadings(key, width):
    phase_key, rough_key = jax.random.split(key)
    phase = jax.random.uniform(phase_key, (6, 1))
    cycles = (1.0 + jnp.arange(6, dtype=jnp.float32) % 3.0)[:, None]
    position = jnp.arange(width, dtype=jnp.float32)[None, :] / width
    envelope = jnp.exp(jnp.log(3.0) * jnp.sin(2.0 * jnp.pi * (cycles * position + phase)))
    rough = jnp.clip(jax.random.normal(rough_key, (6, width)), -3.0, 3.0)
    return envelope * rough


def coherent(signs, loads):
    total = jnp.zeros((signs.shape[1], loads.shape[1]), jnp.float32)
    for index in range(6):
        total = total + signs[index][:, None] * loads[index][None, :]
    return 0.1 * total


def scaled_panel(key, signs, length, width):
    first_key = jax.random.fold_in(key, 0)
    third_key = jax.random.fold_in(key, 2)
    fifth_key = jax.random.fold_in(key, 4)
    position = jnp.arange(width, dtype=jnp.float32) / (width - 1)
    trend = jnp.exp(0.5 * jnp.log(3.0) * position)
    shared = coherent(signs, loadings(fifth_key, width))
    spread = jnp.exp(jax.random.uniform(first_key, (width,), minval=0.0, maxval=jnp.log(3.0)))
    values = jnp.clip(jax.random.normal(third_key, (length, width)), -4.0, 4.0) + shared
    return (values * (spread * trend)[None, :]).astype(jnp.bfloat16)


def draw_activations(key, part):
    signs = token_signs(jax.random.fold_in(key, 101))
    return scaled_panel(jax.random.fold_in(key, 11), signs, TOKENS, D)


def draw_output_grads(key, part):
    signs = token_signs(jax.random.fold_in(key, 101))
    return scaled_panel(jax.random.fold_in(key, 23), signs, TOKENS, FF)


def plant(values, stream_key, low, largest):
    dims = values.shape
    place = [jax.random.randint(jax.random.fold_in(stream_key, axis), (), 0, dims[axis]) for axis in range(len(dims))]
    values = values.at[tuple(place)].set(low)
    longest = dims.index(max(dims))
    place[longest] = (place[longest] + 1) % dims[longest]
    return values.at[tuple(place)].set(largest)


def block_levels(key, extent, cuts, smallest, top_value):
    level, own = 1.0, jax.random.fold_in(key, 6)
    for dim, parts in cuts:
        heights = jnp.exp(jax.random.uniform(jax.random.fold_in(own, dim), (parts,), jnp.float32, smallest / len(cuts), top_value / len(cuts)))
        level = level * jnp.repeat(heights, extent[dim] // parts).reshape([-1 if axis == dim else 1 for axis in range(len(extent))])
    return level


def setup_inputs(seed: int = 0) -> dict:
    key_of = jax.random.split(jax.random.key(seed), 8)
    activations = draw_activations(jax.random.fold_in(key_of[7], 71), 0)
    output_grads = draw_output_grads(jax.random.fold_in(key_of[7], 71), 0)
    first_codes = plant(jax.random.randint(key_of[2], (D, FF // 2), 0, 256), jax.random.fold_in(key_of[2], 1), 0, 255).astype(jnp.int32)
    second_codes = plant(jax.random.randint(key_of[3], (D, FF // 2), 0, 256), jax.random.fold_in(key_of[3], 1), 0, 255).astype(jnp.int32)
    first_scales = jnp.clip(jnp.exp(math.log(1.0) - 2.3025851 * jax.random.uniform(key_of[4], (D, FF // 128), jnp.float32) ** block_levels(key_of[4], (D, FF // 128), ((0, 32), (1, 8)), -0.2, 0.2)), 0.1, 1.0)
    second_rows = jnp.clip(jnp.exp(math.log(0.3) - 2.3025852 * jax.random.uniform(key_of[5], (D,), jnp.float32) ** block_levels(key_of[5], (D,), ((0, 32),), -0.2, 0.2)), 0.03, 0.3)
    second_cols = jnp.clip(jnp.exp(math.log(0.3) - 2.3025852 * jax.random.uniform(key_of[6], (FF,), jnp.float32) ** block_levels(key_of[6], (FF,), ((0, 8),), -0.2, 0.2)), 0.03, 0.3)
    return {"activations": activations, "output_grads": output_grads, "first_codes": first_codes, "second_codes": second_codes, "first_scales": first_scales, "second_rows": second_rows, "second_cols": second_cols}


bias_one = 1.0 - 0.9 ** 10
bias_two = 1.0 - 0.95 ** 10

def decode(packed):
    height = packed.shape[0]
    low_half = jnp.bitwise_and(packed, 15).reshape(height, -1, 1, 128)
    high_half = jnp.right_shift(packed, 4).reshape(height, -1, 1, 128)
    return jnp.concatenate([low_half, high_half], axis=2).reshape(height, -1, 128).astype(jnp.float32)

def advance(gradient, clip_factor, first_codes, second_codes, first_scales, second_rows, second_cols):
    height = gradient.shape[0]
    scaled = clip_factor * gradient.reshape(height, -1, 128)
    first_old = first_scales[:, :, None] * ((decode(first_codes) - 7.5) / 7.5)
    rank_scale = jnp.minimum(second_rows[:, None], second_cols[None, :]).reshape(height, -1, 128)
    second_old = rank_scale * ((decode(second_codes) + 1.0) / 16.0)
    new_first = 0.9 * first_old + 0.1 * scaled
    new_second = 0.95 * second_old + 0.05 * scaled * scaled
    update = new_first / bias_one / (jnp.sqrt(new_second / bias_two) + 1e-08)
    first_peaks = lax.optimization_barrier(jnp.max(jnp.abs(new_first), axis=2))
    first_normed = (new_first / (first_peaks[:, :, None] + 1e-06)).astype(jnp.bfloat16)
    return (update.reshape(height, -1), first_normed.reshape(height, -1), first_peaks, new_second.reshape(height, -1))

def reference(activations, output_grads, first_codes, second_codes, first_scales, second_rows, second_cols):
    gradient = jnp.dot(activations.T, output_grads, preferred_element_type=jnp.float32)
    sumsq = jnp.sum(gradient * gradient)
    clip_factor = jnp.minimum(1.0, jnp.sqrt(jnp.float32(D * FF) / sumsq))
    height = D // N_ROW

    def stack(array):
        return array.reshape((N_ROW, height) + array.shape[1:])

    def first_pass(blocks):
        grad_block, first_block, second_block, scale_block, peak_block = blocks
        return advance(grad_block, clip_factor, first_block, second_block, scale_block, peak_block, second_cols)
    update, first_normed, first_peaks, new_second = lax.map(first_pass, (stack(gradient), stack(first_codes), stack(second_codes), stack(first_scales), stack(second_rows)))
    row_peaks = lax.optimization_barrier(jnp.max(new_second, axis=2))
    col_peaks = lax.optimization_barrier(jnp.max(new_second, axis=(0, 1)))

    def second_pass(blocks):
        values, peaks = blocks
        return (values / jnp.minimum(peaks[:, None], col_peaks[None, :])).astype(jnp.bfloat16)
    second_normed = lax.map(second_pass, (new_second, row_peaks))
    return (update.reshape(D, FF), first_normed.reshape(D, FF), first_peaks.reshape(D, FF // 128), second_normed.reshape(D, FF), row_peaks.reshape(D), col_peaks)
```

```python
import functools

import jax
import jax.numpy as jnp
from jax import lax
from jax.experimental import pallas as pl
from jax.experimental.pallas import tpu as pltpu
from jax.sharding import PartitionSpec as P

MESH = pl.DeviceIdType.MESH
D = 8192
FF = 24576
TOKENS = 2048
ROWS = 256
COLS = 3072
NZ, NY, NX = 8, 4, 4
PART = COLS // NY
CHUNKS = 6
WIDTH = PART // CHUNKS
LANES = 128
WB = WIDTH // LANES
BLOCKS = COLS // LANES
ZROWS = TOKENS // NZ
TOK = TOKENS // (NZ * NY)

BIAS_ONE = 1.0 - 0.9**10
BIAS_TWO = 1.0 - 0.95**10


class Copies:
    def __init__(self, send, recv):
        self.send, self.recv = send, recv
        self.made = {}

    def start(self, key, src, dst, device):
        slot = len(self.made)
        copy = pltpu.make_async_remote_copy(
            src_ref=src,
            dst_ref=dst,
            send_sem=self.send.at[slot],
            recv_sem=self.recv.at[slot],
            device_id=device,
            device_id_type=MESH,
        )
        copy.start()
        self.made[key] = copy

    def arrived(self, key):
        self.made[key].wait_recv()

    def finish(self):
        for copy in self.made.values():
            copy.wait_send()


def n_copies():
    return CHUNKS * 3 + CHUNKS * 8 + 6 + 24 + 4 + CHUNKS * 3 + 14 + 10 + 4


def gather_kernel(
    act,
    grads,
    codes2_hbm,
    rows,
    cols,
    g_out,
    clip_out,
    rows_out,
    rinv_out,
    rp_out,
    cp_out,
    at,
    bb,
    gs,
    go,
    quad,
    codes2,
    sq,
    ss_src,
    ss_dst,
    cp_a,
    cp_b,
    cp_dst,
    rp_a,
    rp_b,
    rp_dst,
    rowacc,
    colacc,
    send,
    recv,
    local,
):
    r, c = lax.axis_index("row"), lax.axis_index("col")
    z, y = r // NY, r % NY
    x, k = c // 2, c % 2

    def to_z(d):
        return ((z + d + NZ) % NZ * NY + y, c)

    def to_y(d):
        return (z * NY + (y + d) % NY, c)

    def to_x(d):
        return (r, (x + d) % NX * 2 + k)

    peer = (r, x * 2 + 1 - k)

    load = pltpu.make_async_copy(codes2_hbm, codes2, local.at[0])
    load.start()

    barrier = pltpu.get_barrier_semaphore()
    partners = (
        [to_y(d) for d in (1, 3, 2)]
        + [to_x(d) for d in (1, 3, 2)]
        + [peer]
        + [to_z(d) for d in range(1, NZ)]
    )
    for partner in partners:
        pl.semaphore_signal(barrier, inc=1, device_id=partner, device_id_type=MESH)

    def spot(yy, cc, half=None):
        if half is None:
            return at.at[pl.ds(yy * ROWS, ROWS), pl.ds(cc * ROWS, ROWS)]
        size = ROWS // 2
        return at.at[pl.ds(yy * ROWS + half * size, size), pl.ds(cc * ROWS, ROWS)]

    spot(y, c)[...] = act[...].T

    def b_part(n, zz):
        return bb.at[n, pl.ds(zz * ZROWS, ZROWS)]

    owns = []
    for n in range(CHUNKS):
        own = pltpu.make_async_copy(
            grads.at[:, pl.ds(y * PART + n * WIDTH, WIDTH)],
            bb.at[n, pl.ds(z * ZROWS + y * TOK, TOK)],
            local.at[2 + n],
        )
        own.start()
        owns.append(own)
    pl.semaphore_wait(barrier, len(partners))

    net = Copies(send, recv)
    ring = (1, 3, 2)

    def spread(n):
        for d in ring:
            other = (y + d) % NY
            net.start(
                ("b1", n, d),
                grads.at[:, pl.ds(other * PART + n * WIDTH, WIDTH)],
                bb.at[n, pl.ds(z * ZROWS + y * TOK, TOK)],
                to_y(d),
            )

    def pass_on(n, s):
        if s == 1:
            owns[n].wait()
            for d in ring:
                net.arrived(("b1", n, d))
        for way in (1, -1):
            if s > 1:
                net.arrived(("b2", n, s - 1, way))
            zz = (z - way * (s - 1) + NZ) % NZ
            if s < 4:
                ref = b_part(n, zz)
            else:
                half = ZROWS // 2
                ref = bb.at[n, pl.ds(zz * ZROWS + (half if way < 0 else 0), half)]
            net.start(("b2", n, s, way), ref, ref, to_z(way))

    spread(0)
    for d in ring:
        ref = spot(y, c, 0)
        net.start(("ay", 0, d), ref, ref, to_y(d))
        ref = spot(y, c, 1)
        net.start(("ax", 0, d), ref, ref, to_x(d))
    for d in ring:
        ref = spot(y, c, 0)
        net.start(("axy", 0, d), ref, ref, to_x(d))
    spread(1)
    for d in ring:
        ref = spot(y, c, 1)
        net.start(("ayx", 0, d), ref, ref, to_y(d))
    for n in range(2, CHUNKS):
        spread(n)
    pass_on(0, 1)
    for e in ring:
        net.arrived(("ay", 0, e))
        ref = spot((y + NY - e) % NY, c, 0)
        for d in ring:
            net.start(("axy", e, d), ref, ref, to_x(d))
        net.arrived(("ax", 0, e))
        ref = spot(y, (x + NX - e) % NX * 2 + k, 1)
        for d in ring:
            net.start(("ayx", e, d), ref, ref, to_y(d))

    def to_peer(q):
        if q == 0:
            for d in ring:
                net.arrived(("ayx", 0, d))
        else:
            for e in (0,) + ring:
                net.arrived(("axy", e, q))
            for d in ring:
                net.arrived(("ayx", q, d))
        ref = at.at[:, pl.ds(((x + NX - q) % NX * 2 + k) * ROWS, ROWS)]
        net.start(("peer", q), ref, ref, peer)

    def decode_second():
        load.wait()
        spread_rows = jnp.broadcast_to(rows[...].reshape(1, ROWS), (LANES, ROWS)).T
        rows_out[...] = spread_rows

        def body(i, carry):
            at_rows = pl.ds(pl.multiple_of(i * 32, 32), 32)
            row = rows_out[at_rows, :] * (0.95 / 16.0)
            for w in range(BLOCKS // 2):
                word = codes2[at_rows, pl.ds(w * LANES, LANES)]
                for h in range(2):
                    b = 2 * w + h
                    code = word & 15 if h == 0 else word >> 4
                    col = cols[pl.ds(b * LANES, LANES)].reshape(1, LANES) * (0.95 / 16.0)
                    quad[b, at_rows, :] = jnp.minimum(row, col) * (code.astype(jnp.float32) + 1.0)
            return carry

        lax.fori_loop(0, ROWS // 32, body, 0)

    sq[...] = jnp.zeros_like(sq)

    def multiply(n):
        for d in (2, 1, 3, 0):
            other = (y + d) % NY
            res = jnp.dot(
                at[pl.ds(pl.multiple_of(other * ROWS, ROWS), ROWS), :],
                bb[n],
                preferred_element_type=jnp.float32,
            )
            sq[...] += jnp.sum((res * res).reshape(ROWS // 8, 8, WIDTH), axis=0)
            place = pl.ds(y * (PART // LANES) + n * WB, WB)
            for w in range(WB):
                piece = res[:, w * LANES : (w + 1) * LANES]
                if d:
                    gs[n, d - 1, w] = piece
                else:
                    go[y * (PART // LANES) + n * WB + w] = piece
            if d:
                net.start(("out", n, d), gs.at[n, d - 1], go.at[place], to_y(d))

    extra = {
        2: [decode_second],
        4: [lambda: to_peer(0)],
        5: [lambda: to_peer(1), lambda: to_peer(3), lambda: to_peer(2)],
    }
    done = 0
    for slot in range(2, CHUNKS + 5):
        for n in range(CHUNKS):
            s = slot - n
            if 1 <= s <= 4 and (n, s) != (0, 1):
                pass_on(n, s)
        for step in extra.get(slot, ()):
            step()
        if slot >= 6 or slot == CHUNKS + 4:
            last = slot == CHUNKS + 4
            upto = CHUNKS if last else slot - 5
            if done == 0:
                for q in (0,) + ring:
                    net.arrived(("peer", q))
            while done < upto:
                for way in (1, -1):
                    net.arrived(("b2", done, 4, way))
                multiply(done)
                done += 1

    ss_src[0] = jnp.full((8, LANES), jnp.sum(sq[...]))
    slot = 0
    stages = [
        [("ss", 0, 0, peer)],
        [("ss", 1, d, to_x(d)) for d in ring],
        [("ss", 2, d, to_y(d)) for d in ring],
        [("ss", 3, d, to_z(d)) for d in range(1, NZ)],
    ]
    for i, stage in enumerate(stages):
        for j, (name, _, d, device) in enumerate(stage):
            net.start((name, i, d), ss_src.at[i], ss_dst.at[slot + j], device)
        total = ss_src[i]
        for j, (name, _, d, device) in enumerate(stage):
            net.arrived((name, i, d))
            total = total + ss_dst[slot + j]
        slot += len(stage)
        if i < 3:
            ss_src[i + 1] = total
    limit = float(D) * FF
    clip = jnp.where(total <= limit, 1.0, jnp.sqrt(limit / jnp.maximum(total, limit)))
    clip_out[...] = clip

    for n in range(CHUNKS):
        for d in ring:
            net.arrived(("out", n, d))
    save = pltpu.make_async_copy(go, g_out, local.at[1])
    save.start()

    rate = clip[0:1, :]
    colacc[...] = jnp.zeros_like(colacc)

    def body(i, carry):
        at_rows = pl.ds(pl.multiple_of(i * 32, 32), 32)
        best = jnp.zeros((32, LANES), jnp.float32)
        for b in range(BLOCKS):
            scaled = rate * go[b, at_rows, :]
            second = quad[b, at_rows, :] + 0.05 * scaled * scaled
            best = jnp.maximum(best, second)
            colacc[b] = jnp.maximum(colacc[b], jnp.max(second.reshape(4, 8, LANES), axis=0))
        rowacc[at_rows, :] = best
        return carry

    lax.fori_loop(0, ROWS // 32, body, 0)
    rp_a[...] = jnp.broadcast_to(
        jnp.max(rowacc[...].T, axis=0, keepdims=True), (8, ROWS)
    )
    for b in range(BLOCKS):
        cp_a[b : b + 1, :] = jnp.max(colacc[b], axis=0, keepdims=True)

    for j, d in enumerate(ring):
        net.start(("cy", d), cp_a, cp_dst.at[j], to_y(d))
    net.start(("rk",), rp_a, rp_dst.at[0], peer)
    net.arrived(("rk",))
    rp_b[...] = jnp.maximum(rp_a[...], rp_dst[0])
    for j, d in enumerate(ring):
        net.start(("rx", d), rp_b, rp_dst.at[1 + j], to_x(d))
    for d in ring:
        net.arrived(("cy", d))
    cp_b[...] = jnp.maximum(
        jnp.maximum(cp_a[...], cp_dst[0]), jnp.maximum(cp_dst[1], cp_dst[2])
    )
    for d in range(1, NZ):
        net.start(("cz", d), cp_b, cp_dst.at[2 + d], to_z(d))
    peaks = rp_b[...]
    for j, d in enumerate(ring):
        net.arrived(("rx", d))
        peaks = jnp.maximum(peaks, rp_dst[1 + j])
    rp_out[...] = peaks
    rinv_out[...] = jnp.broadcast_to((1.0 / peaks)[0:1, :], (LANES, ROWS)).T
    tops = cp_b[...]
    for d in range(1, NZ):
        net.arrived(("cz", d))
        tops = jnp.maximum(tops, cp_dst[2 + d])
    cp_out[...] = tops
    save.wait()
    net.finish()


def adam_kernel(
    g,
    clip,
    codes1,
    codes2,
    scales,
    row_scale,
    cols,
    row_inv,
    rp,
    cp,
    update,
    first_normed,
    first_peaks,
    second_normed,
    row_peaks,
    col_peaks,
    cinv,
):
    @pl.when(pl.program_id(0) == 0)
    def _():
        row_peaks[...] = rp[0:1, :].reshape(ROWS)
        for b in range(BLOCKS):
            col_peaks[pl.ds(b * LANES, LANES)] = cp[b : b + 1, :].reshape(LANES)
        cinv[...] = 1.0 / cp[...]

    height = codes1.shape[0]
    rate = clip[0:1, :]
    lane = lax.broadcasted_iota(jnp.int32, (height, LANES), 1)
    row = row_scale[...] * (0.95 / 16.0)
    rinv = row_inv[...]
    peaks = jnp.zeros((height, LANES), jnp.float32)
    for b in range(BLOCKS):
        at_word = pl.ds(b // 2 * LANES, LANES)
        at_cols = pl.ds(b * LANES, LANES)

        def code(ref):
            word = ref[:, at_word]
            return (word & 15 if b % 2 == 0 else word >> 4).astype(jnp.float32)

        scaled = rate * g[b]
        first = (scales[:, b : b + 1] * (0.9 / 7.5)) * (code(codes1) - 7.5) + 0.1 * scaled
        col = cols[at_cols].reshape(1, LANES) * (0.95 / 16.0)
        second = jnp.minimum(row, col) * (code(codes2) + 1.0) + 0.05 * scaled * scaled
        peak = jnp.max(jnp.abs(first), axis=1, keepdims=True)
        peaks = jnp.where(lane == b, peak, peaks)
        first_normed[:, at_cols] = (first * (1.0 / (peak + 1e-06))).astype(jnp.bfloat16)
        under = second * (1.0 / BIAS_TWO)
        root = under * lax.rsqrt(under)
        update[:, at_cols] = (first * (1.0 / BIAS_ONE)) / (root + 1e-08)
        second_normed[:, at_cols] = (second * jnp.maximum(rinv, cinv[b : b + 1, :])).astype(
            jnp.bfloat16
        )
    first_peaks[...] = peaks[:, :BLOCKS]


def local(activations, output_grads, first_codes, second_codes, first_scales, second_rows, second_cols):
    f32, bf16 = jnp.float32, jnp.bfloat16
    vmem = pl.BlockSpec(memory_space=pltpu.VMEM)
    hbm = pl.BlockSpec(memory_space=pl.ANY)
    g, clip, row_scale, row_inv, rp, cp = pl.pallas_call(
        gather_kernel,
        out_shape=(
            jax.ShapeDtypeStruct((BLOCKS, ROWS, LANES), f32),
            jax.ShapeDtypeStruct((8, LANES), f32),
            jax.ShapeDtypeStruct((ROWS, LANES), f32),
            jax.ShapeDtypeStruct((ROWS, LANES), f32),
            jax.ShapeDtypeStruct((8, ROWS), f32),
            jax.ShapeDtypeStruct((BLOCKS, LANES), f32),
        ),
        in_specs=[vmem, vmem, hbm, vmem, vmem],
        out_specs=(hbm, vmem, vmem, vmem, vmem, vmem),
        scratch_shapes=[
            pltpu.VMEM((NY * ROWS, TOKENS), bf16),
            pltpu.VMEM((CHUNKS, TOKENS, WIDTH), bf16),
            pltpu.VMEM((CHUNKS, 3, WB, ROWS, LANES), f32),
            pltpu.VMEM((BLOCKS, ROWS, LANES), f32),
            pltpu.VMEM((BLOCKS, ROWS, LANES), f32),
            pltpu.VMEM((ROWS, COLS // 2), jnp.int32),
            pltpu.VMEM((8, WIDTH), f32),
            pltpu.VMEM((4, 8, LANES), f32),
            pltpu.VMEM((14, 8, LANES), f32),
            pltpu.VMEM((BLOCKS, LANES), f32),
            pltpu.VMEM((BLOCKS, LANES), f32),
            pltpu.VMEM((10, BLOCKS, LANES), f32),
            pltpu.VMEM((8, ROWS), f32),
            pltpu.VMEM((8, ROWS), f32),
            pltpu.VMEM((4, 8, ROWS), f32),
            pltpu.VMEM((ROWS, LANES), f32),
            pltpu.VMEM((BLOCKS, 8, LANES), f32),
            pltpu.SemaphoreType.DMA((n_copies(),)),
            pltpu.SemaphoreType.DMA((n_copies(),)),
            pltpu.SemaphoreType.DMA((2 + CHUNKS,)),
        ],
        compiler_params=pltpu.CompilerParams(
            collective_id=0, has_side_effects=True, vmem_limit_bytes=48 * 2**20
        ),
        name="gather",
    )(activations, output_grads, second_codes, second_rows, second_cols)

    tile = 32

    def by_rows(*shape):
        return pl.BlockSpec(shape, lambda i: (i, 0))

    def whole(*shape):
        return pl.BlockSpec(shape, lambda i: (0,) * len(shape))

    return pl.pallas_call(
        adam_kernel,
        grid=(ROWS // tile,),
        out_shape=(
            jax.ShapeDtypeStruct((ROWS, COLS), f32),
            jax.ShapeDtypeStruct((ROWS, COLS), bf16),
            jax.ShapeDtypeStruct((ROWS, BLOCKS), f32),
            jax.ShapeDtypeStruct((ROWS, COLS), bf16),
            jax.ShapeDtypeStruct((ROWS,), f32),
            jax.ShapeDtypeStruct((COLS,), f32),
        ),
        in_specs=[
            pl.BlockSpec((BLOCKS, tile, LANES), lambda i: (0, i, 0)),
            whole(8, LANES),
            by_rows(tile, COLS // 2),
            by_rows(tile, COLS // 2),
            by_rows(tile, BLOCKS),
            by_rows(tile, LANES),
            whole(COLS),
            by_rows(tile, LANES),
            whole(8, ROWS),
            whole(BLOCKS, LANES),
        ],
        out_specs=(
            by_rows(tile, COLS),
            by_rows(tile, COLS),
            by_rows(tile, BLOCKS),
            by_rows(tile, COLS),
            whole(ROWS),
            whole(COLS),
        ),
        scratch_shapes=[pltpu.VMEM((BLOCKS, LANES), f32)],
        compiler_params=pltpu.CompilerParams(vmem_limit_bytes=32 * 2**20),
        name="adam",
    )(g, clip, first_codes, second_codes, first_scales, row_scale, second_cols, row_inv, rp, cp)


def solution(mesh):
    return jax.shard_map(
        local,
        mesh=mesh,
        in_specs=(
            P("col", "row"),
            P("row", "col"),
            P("row", "col"),
            P("row", "col"),
            P("row", "col"),
            P("row"),
            P("col"),
        ),
        out_specs=(
            P("row", "col"),
            P("row", "col"),
            P("row", "col"),
            P("row", "col"),
            P("row"),
            P("col"),
        ),
        check_vma=False,
    )
```

```python
import jax
import jax.numpy as jnp
from jax import lax
from jax.experimental import pallas as pl
from jax.experimental.pallas import tpu as pltpu
from jax.sharding import PartitionSpec as P

MESH = pl.DeviceIdType.MESH
D = 8192
FF = 24576
TOKENS = 2048
ROWS = 256
COLS = 3072
NZ, NY, NX = 8, 4, 4
PART = COLS // NY
CHUNKS = 6
WIDTH = PART // CHUNKS
LANES = 128
TILE = 32
FINISH = 64
BLOCKS = COLS // LANES
ZROWS = TOKENS // NZ
TOK = TOKENS // (NZ * NY)

BIAS_ONE = 1.0 - 0.9**10
BIAS_TWO = 1.0 - 0.95**10


class Copies:
    def __init__(self, send, recv):
        self.send, self.recv = send, recv
        self.made = {}

    def start(self, key, src, dst, device):
        slot = len(self.made)
        copy = pltpu.make_async_remote_copy(
            src_ref=src,
            dst_ref=dst,
            send_sem=self.send.at[slot],
            recv_sem=self.recv.at[slot],
            device_id=device,
            device_id_type=MESH,
        )
        copy.start()
        self.made[key] = copy

    def arrived(self, key):
        self.made[key].wait_recv()

    def finish(self):
        for copy in self.made.values():
            copy.wait_send()


def n_copies():
    return CHUNKS * (3 + 8 + 3 + 3) + 6 + 24 + 4 + 14 + 10 + 4


def step_kernel(
    act_hbm,
    grads,
    codes1_hbm,
    codes2_hbm,
    scales_hbm,
    rows_hbm,
    cols_hbm,
    update,
    first_normed,
    first_peaks,
    second,
    rinv_out,
    rp_out,
    cp_out,
    act,
    codes1,
    codes2,
    scales,
    rows,
    cols,
    at,
    bb,
    gs,
    gs_scale,
    gi,
    gi_scale,
    mom,
    sq,
    ss_src,
    ss_dst,
    cp_a,
    cp_b,
    cp_dst,
    rp_a,
    rp_b,
    rp_dst,
    rowacc,
    colacc,
    send,
    recv,
    local,
):
    r, c = lax.axis_index("row"), lax.axis_index("col")
    z, y = r // NY, r % NY
    x, k = c // 2, c % 2

    def to_z(d):
        return ((z + d + NZ) % NZ * NY + y, c)

    def to_y(d):
        return (z * NY + (y + d) % NY, c)

    def to_x(d):
        return (r, (x + d) % NX * 2 + k)

    peer = (r, x * 2 + 1 - k)

    barrier = pltpu.get_barrier_semaphore()
    partners = (
        [to_z(d) for d in range(1, NZ)]
        + [to_y(d) for d in (1, 3, 2)]
        + [to_x(d) for d in (1, 3, 2)]
        + [peer]
    )
    for partner in partners:
        pl.semaphore_signal(barrier, inc=1, device_id=partner, device_id_type=MESH)

    pairs = (
        (act_hbm, act),
        (codes2_hbm, codes2),
        (rows_hbm, rows),
        (cols_hbm, cols),
        (scales_hbm, scales),
        (codes1_hbm, codes1),
    )
    loads = [pltpu.make_async_copy(src, dst, local.at[i]) for i, (src, dst) in enumerate(pairs)]
    for load in loads:
        load.start()

    def spot(yy, cc, half=None):
        if half is None:
            return at.at[pl.ds(yy * ROWS, ROWS), pl.ds(cc * ROWS, ROWS)]
        size = ROWS // 2
        return at.at[pl.ds(yy * ROWS + half * size, size), pl.ds(cc * ROWS, ROWS)]

    def b_part(n, zz):
        return bb.at[n, pl.ds(zz * ZROWS, ZROWS)]

    owns = []
    for n in range(CHUNKS):
        own = pltpu.make_async_copy(
            grads.at[:, pl.ds(y * PART + n * WIDTH, WIDTH)],
            bb.at[n, pl.ds(z * ZROWS + y * TOK, TOK)],
            local.at[len(pairs) + n],
        )
        own.start()
        owns.append(own)
    loads[0].wait()
    spot(y, c)[...] = act[...].T

    def decode_second():
        for load in loads[1:4]:
            load.wait()
        rowacc[...] = jnp.broadcast_to(rows[...].reshape(1, ROWS), (LANES, ROWS)).T * (0.95 / 16.0)

        @pl.loop(0, ROWS // TILE)
        def _(i):
            at_rows = pl.ds(pl.multiple_of(i * TILE, TILE), TILE)
            row = rowacc[at_rows, :]
            for b in range(BLOCKS):
                word = codes2[at_rows, pl.ds(b // 2 * LANES, LANES)]
                code = word & 15 if b % 2 == 0 else word >> 4
                col = cols[pl.ds(b * LANES, LANES)].reshape(1, LANES) * (0.95 / 16.0)
                second[b, at_rows, :] = jnp.minimum(row, col) * (code.astype(jnp.float32) + 1.0)

    def decode_first():
        for load in loads[4:]:
            load.wait()
        wide = jnp.concatenate(
            [scales[...], jnp.zeros((LANES - BLOCKS, ROWS), jnp.float32)], axis=0
        )
        rowacc[...] = wide.T * (0.9 / 7.5)

        @pl.loop(0, ROWS // TILE)
        def _(i):
            at_rows = pl.ds(pl.multiple_of(i * TILE, TILE), TILE)
            scale = rowacc[at_rows, :]
            for b in range(BLOCKS):
                word = codes1[at_rows, pl.ds(b // 2 * LANES, LANES)]
                code = word & 15 if b % 2 == 0 else word >> 4
                mom[b, at_rows, :] = scale[:, b : b + 1] * (code.astype(jnp.float32) - 7.5)

    decode_second()
    pl.semaphore_wait(barrier, len(partners))

    net = Copies(send, recv)
    ring = (1, 3, 2)

    def spread(n):
        for d in ring:
            other = (y + d) % NY
            net.start(
                ("b1", n, d),
                grads.at[:, pl.ds(other * PART + n * WIDTH, WIDTH)],
                bb.at[n, pl.ds(z * ZROWS + y * TOK, TOK)],
                to_y(d),
            )

    def pass_on(n, s):
        if s == 1:
            owns[n].wait()
            for d in ring:
                net.arrived(("b1", n, d))
        for way in (1, -1):
            if s > 1:
                net.arrived(("b2", n, s - 1, way))
            zz = (z - way * (s - 1) + NZ) % NZ
            if s < 4:
                ref = b_part(n, zz)
            else:
                half = ZROWS // 2
                ref = bb.at[n, pl.ds(zz * ZROWS + (half if way < 0 else 0), half)]
            net.start(("b2", n, s, way), ref, ref, to_z(way))

    spread(0)
    for d in ring:
        ref = spot(y, c, 0)
        net.start(("ay", 0, d), ref, ref, to_y(d))
        ref = spot(y, c, 1)
        net.start(("ax", 0, d), ref, ref, to_x(d))
    for d in ring:
        ref = spot(y, c, 0)
        net.start(("axy", 0, d), ref, ref, to_x(d))
    spread(1)
    for d in ring:
        ref = spot(y, c, 1)
        net.start(("ayx", 0, d), ref, ref, to_y(d))
    for n in range(2, CHUNKS):
        spread(n)
    decode_first()
    pass_on(0, 1)
    for e in ring:
        net.arrived(("ay", 0, e))
        ref = spot((y + NY - e) % NY, c, 0)
        for d in ring:
            net.start(("axy", e, d), ref, ref, to_x(d))
        net.arrived(("ax", 0, e))
        ref = spot(y, (x + NX - e) % NX * 2 + k, 1)
        for d in ring:
            net.start(("ayx", e, d), ref, ref, to_y(d))

    def to_peer(q):
        if q == 0:
            for d in ring:
                net.arrived(("ayx", 0, d))
        else:
            for e in (0,) + ring:
                net.arrived(("axy", e, q))
            for d in ring:
                net.arrived(("ayx", q, d))
        ref = at.at[:, pl.ds(((x + NX - q) % NX * 2 + k) * ROWS, ROWS)]
        net.start(("peer", q), ref, ref, peer)

    sq[...] = jnp.zeros_like(sq)

    def multiply(n):
        for d in (2, 1, 3, 0):
            other = (y + d) % NY
            res = jnp.dot(
                at[pl.ds(pl.multiple_of(other * ROWS, ROWS), ROWS), :],
                bb[n],
                preferred_element_type=jnp.float32,
            )
            tiles = res.reshape(ROWS // 8, 8, WIDTH)
            sq[...] += jnp.sum(tiles * tiles, axis=0)
            top = jnp.max(jnp.max(jnp.abs(tiles), axis=0), axis=0, keepdims=True)
            top = jnp.maximum(top, 1e-30)
            words = jnp.round(res * (32767.0 / top)).astype(jnp.int32).astype(jnp.int16)
            scale = jnp.broadcast_to(top * (1.0 / 32767.0), (8, LANES))
            block = y * (PART // LANES) + n
            if d:
                gs[n, d - 1] = words
                gs_scale[n, d - 1] = scale
                net.start(("out", n, d), gs.at[n, d - 1], gi.at[block], to_y(d))
                net.start(("scale", n, d), gs_scale.at[n, d - 1], gi_scale.at[block], to_y(d))
            else:
                gi[block] = words
                gi_scale[block] = scale

    extra = {
        4: [lambda: to_peer(0)],
        5: [lambda: to_peer(1), lambda: to_peer(3), lambda: to_peer(2)],
    }
    done = 0
    for slot in range(2, CHUNKS + 5):
        for n in range(CHUNKS):
            s = slot - n
            if 1 <= s <= 4 and (n, s) != (0, 1):
                pass_on(n, s)
        for step in extra.get(slot, ()):
            step()
        if slot >= 6 or slot == CHUNKS + 4:
            last = slot == CHUNKS + 4
            upto = CHUNKS if last else slot - 5
            if done == 0:
                for q in (0,) + ring:
                    net.arrived(("peer", q))
            while done < upto:
                for way in (1, -1):
                    net.arrived(("b2", done, 4, way))
                multiply(done)
                done += 1

    ss_src[0] = jnp.full((8, LANES), jnp.sum(sq[...]))
    slot = 0
    stages = [
        [(0, peer)],
        [(d, to_x(d)) for d in ring],
        [(d, to_y(d)) for d in ring],
        [(d, to_z(d)) for d in range(1, NZ)],
    ]
    for i, stage in enumerate(stages):
        for j, (d, device) in enumerate(stage):
            net.start(("ss", i, d), ss_src.at[i], ss_dst.at[slot + j], device)
        total = ss_src[i]
        for j, (d, device) in enumerate(stage):
            net.arrived(("ss", i, d))
            total = total + ss_dst[slot + j]
        slot += len(stage)
        if i < 3:
            ss_src[i + 1] = total
    limit = float(D) * FF
    clip = jnp.where(total <= limit, 1.0, jnp.sqrt(limit / jnp.maximum(total, limit)))

    for n in range(CHUNKS):
        for d in ring:
            net.arrived(("out", n, d))
            net.arrived(("scale", n, d))

    rate = clip[0:1, :]
    colacc[...] = jnp.zeros_like(colacc)

    @pl.loop(0, ROWS // TILE)
    def _(i):
        at_rows = pl.ds(pl.multiple_of(i * TILE, TILE), TILE)
        best = jnp.zeros((TILE, LANES), jnp.float32)
        for b in range(BLOCKS):
            words = gi[b, at_rows, :].astype(jnp.int32).astype(jnp.float32)
            scaled = words * (gi_scale[b, 0:1, :] * rate)
            value = second[b, at_rows, :] + 0.05 * scaled * scaled
            second[b, at_rows, :] = value
            mom[b, at_rows, :] += 0.1 * scaled
            best = jnp.maximum(best, value)
            colacc[b] = jnp.maximum(colacc[b], jnp.max(value.reshape(TILE // 8, 8, LANES), axis=0))
        rowacc[at_rows, :] = best

    for b in range(BLOCKS):
        cp_a[b : b + 1, :] = jnp.max(colacc[b], axis=0, keepdims=True)
    for j, d in enumerate(ring):
        net.start(("cy", d), cp_a, cp_dst.at[j], to_y(d))
    rp_a[...] = jnp.broadcast_to(jnp.max(rowacc[...].T, axis=0, keepdims=True), (8, ROWS))
    net.start(("rk",), rp_a, rp_dst.at[0], peer)

    def advance(first, last):
        lane = lax.broadcasted_iota(jnp.int32, (TILE, LANES), 1)

        @pl.loop(first, last)
        def _(i):
            at_rows = pl.ds(pl.multiple_of(i * TILE, TILE), TILE)
            peaks = jnp.zeros((TILE, LANES), jnp.float32)
            for b in range(BLOCKS):
                at_cols = pl.ds(b * LANES, LANES)
                value = mom[b, at_rows, :]
                peak = jnp.max(jnp.abs(value), axis=1, keepdims=True)
                peaks = jnp.where(lane == b, peak, peaks)
                first_normed[at_rows, at_cols] = (value * inverse(peak + 1e-06)).astype(
                    jnp.bfloat16
                )
                under = second[b, at_rows, :] * (1.0 / BIAS_TWO)
                root = under * lax.rsqrt(under) + 1e-08
                update[at_rows, at_cols] = (value * (1.0 / BIAS_ONE)) * inverse(root)
            rowacc[at_rows, :] = peaks

    advance(0, 3)
    net.arrived(("rk",))
    rp_b[...] = jnp.maximum(rp_a[...], rp_dst[0])
    for j, d in enumerate(ring):
        net.start(("rx", d), rp_b, rp_dst.at[1 + j], to_x(d))
    for d in ring:
        net.arrived(("cy", d))
    cp_b[...] = jnp.maximum(
        jnp.maximum(cp_a[...], cp_dst[0]), jnp.maximum(cp_dst[1], cp_dst[2])
    )
    for d in (4, 3, 5, 2, 6, 1, 7):
        net.start(("cz", d), cp_b, cp_dst.at[2 + d], to_z(d))
    advance(3, ROWS // TILE)
    first_peaks[...] = rowacc[...].T[:BLOCKS, :]
    peaks = rp_b[...]
    for j, d in enumerate(ring):
        net.arrived(("rx", d))
        peaks = jnp.maximum(peaks, rp_dst[1 + j])
    rp_out[...] = peaks
    rinv_out[...] = jnp.broadcast_to((1.0 / peaks)[0:1, :], (LANES, ROWS)).T
    tops = cp_b[...]
    for d in range(1, NZ):
        net.arrived(("cz", d))
        tops = jnp.maximum(tops, cp_dst[2 + d])
    cp_out[...] = tops
    net.finish()


def inverse(value):
    guess = pltpu.reciprocal(value, approx=True)
    return guess * (2.0 - value * guess)


def finish_kernel(
    update_in,
    first_in,
    peaks_in,
    second,
    rinv,
    rp,
    cp,
    update,
    first_normed,
    first_peaks,
    second_normed,
    row_peaks,
    col_peaks,
    normed,
    sems,
):
    copies = [
        pltpu.make_async_copy(update_in, update, sems.at[0]),
        pltpu.make_async_copy(first_in, first_normed, sems.at[1]),
        pltpu.make_async_copy(peaks_in, first_peaks, sems.at[2]),
    ]
    for copy in copies:
        copy.start()
    row_peaks[...] = rp[0:1, :].reshape(ROWS)
    for b in range(BLOCKS):
        col_peaks[pl.ds(b * LANES, LANES)] = cp[b : b + 1, :].reshape(LANES)
    cinv = 1.0 / cp[...]
    for i in range(ROWS // FINISH):
        at_rows = pl.ds(i * FINISH, FINISH)
        for b in range(BLOCKS):
            normed[at_rows, pl.ds(b * LANES, LANES)] = (
                second[b, at_rows, :] * jnp.maximum(rinv[at_rows, :], cinv[b : b + 1, :])
            ).astype(jnp.bfloat16)
        copy = pltpu.make_async_copy(
            normed.at[at_rows], second_normed.at[at_rows], sems.at[3 + i]
        )
        copy.start()
        copies.append(copy)
    for copy in copies:
        copy.wait()


def local(activations, output_grads, first_codes, second_codes, first_scales, second_rows, second_cols):
    f32, bf16 = jnp.float32, jnp.bfloat16
    vmem = pl.BlockSpec(memory_space=pltpu.VMEM)
    hbm = pl.BlockSpec(memory_space=pltpu.HBM)
    update, first_normed, first_peaks, second, rinv, rp, cp = pl.pallas_call(
        step_kernel,
        out_shape=(
            jax.ShapeDtypeStruct((ROWS, COLS), f32),
            jax.ShapeDtypeStruct((ROWS, COLS), bf16),
            jax.ShapeDtypeStruct((BLOCKS, ROWS), f32),
            jax.ShapeDtypeStruct((BLOCKS, ROWS, LANES), f32),
            jax.ShapeDtypeStruct((ROWS, LANES), f32),
            jax.ShapeDtypeStruct((8, ROWS), f32),
            jax.ShapeDtypeStruct((BLOCKS, LANES), f32),
        ),
        in_specs=[hbm] * 7,
        out_specs=(vmem,) * 7,
        scratch_shapes=[
            pltpu.VMEM((ROWS, ROWS), bf16),
            pltpu.VMEM((ROWS, COLS // 2), jnp.int32),
            pltpu.VMEM((ROWS, COLS // 2), jnp.int32),
            pltpu.VMEM((BLOCKS, ROWS), f32),
            pltpu.VMEM((ROWS,), f32),
            pltpu.VMEM((COLS,), f32),
            pltpu.VMEM((NY * ROWS, TOKENS), bf16),
            pltpu.VMEM((CHUNKS, TOKENS, WIDTH), bf16),
            pltpu.VMEM((CHUNKS, 3, ROWS, LANES), jnp.int16),
            pltpu.VMEM((CHUNKS, 3, 8, LANES), f32),
            pltpu.VMEM((BLOCKS, ROWS, LANES), jnp.int16),
            pltpu.VMEM((BLOCKS, 8, LANES), f32),
            pltpu.VMEM((BLOCKS, ROWS, LANES), f32),
            pltpu.VMEM((8, WIDTH), f32),
            pltpu.VMEM((4, 8, LANES), f32),
            pltpu.VMEM((14, 8, LANES), f32),
            pltpu.VMEM((BLOCKS, LANES), f32),
            pltpu.VMEM((BLOCKS, LANES), f32),
            pltpu.VMEM((10, BLOCKS, LANES), f32),
            pltpu.VMEM((8, ROWS), f32),
            pltpu.VMEM((8, ROWS), f32),
            pltpu.VMEM((4, 8, ROWS), f32),
            pltpu.VMEM((ROWS, LANES), f32),
            pltpu.VMEM((BLOCKS, 8, LANES), f32),
            pltpu.SemaphoreType.DMA((n_copies(),)),
            pltpu.SemaphoreType.DMA((n_copies(),)),
            pltpu.SemaphoreType.DMA((6 + CHUNKS,)),
        ],
        compiler_params=pltpu.CompilerParams(
            collective_id=0, has_side_effects=True, vmem_limit_bytes=40 * 2**20
        ),
        name="step",
    )(
        *(
            pltpu.with_memory_space_constraint(array, pltpu.HBM)
            for array in (
                activations,
                output_grads,
                first_codes,
                second_codes,
                first_scales.T,
                second_rows,
                second_cols,
            )
        )
    )
    update, first_normed, first_peaks, second_normed, row_peaks, col_peaks = pl.pallas_call(
        finish_kernel,
        out_shape=(
            jax.ShapeDtypeStruct((ROWS, COLS), f32),
            jax.ShapeDtypeStruct((ROWS, COLS), bf16),
            jax.ShapeDtypeStruct((BLOCKS, ROWS), f32),
            jax.ShapeDtypeStruct((ROWS, COLS), bf16),
            jax.ShapeDtypeStruct((ROWS,), f32),
            jax.ShapeDtypeStruct((COLS,), f32),
        ),
        in_specs=[vmem] * 7,
        out_specs=(hbm, hbm, hbm, hbm, vmem, vmem),
        scratch_shapes=[
            pltpu.VMEM((ROWS, COLS), bf16),
            pltpu.SemaphoreType.DMA((3 + ROWS // FINISH,)),
        ],
        compiler_params=pltpu.CompilerParams(vmem_limit_bytes=16 * 2**20),
        name="finish",
    )(update, first_normed, first_peaks, second, rinv, rp, cp)
    return update, first_normed, first_peaks.T, second_normed, row_peaks, col_peaks


def solution(mesh):
    return jax.shard_map(
        local,
        mesh=mesh,
        in_specs=(
            P("col", "row"),
            P("row", "col"),
            P("row", "col"),
            P("row", "col"),
            P("row", "col"),
            P("row"),
            P("col"),
        ),
        out_specs=(
            P("row", "col"),
            P("row", "col"),
            P("row", "col"),
            P("row", "col"),
            P("row"),
            P("col"),
        ),
        check_vma=False,
    )
```

```python
import jax
import jax.numpy as jnp
from jax import lax
from jax.experimental import pallas as pl
from jax.experimental.pallas import tpu as pltpu
from jax.sharding import PartitionSpec as P

MESH = pl.DeviceIdType.MESH
D = 8192
FF = 24576
TOKENS = 2048
ROWS = 256
COLS = 3072
NZ, NY, NX = 8, 4, 4
PART = COLS // NY
CHUNKS = 2
WIDTH = PART // CHUNKS
LANES = 128
WB = WIDTH // LANES
TILE = 32
FINISH = 64
BLOCKS = COLS // LANES
ZROWS = TOKENS // NZ
FAR = TOKENS - ZROWS
PIECES = ((0, 96), (96, 80), (176, 80))
HALF_PIECES = ((0, 48), (48, 48), (96, 32))
TOK = TOKENS // (NZ * NY)

BIAS_ONE = 1.0 - 0.9**10
BIAS_TWO = 1.0 - 0.95**10


class Copies:
    def __init__(self, send, recv):
        self.send, self.recv = send, recv
        self.made = {}

    def start(self, key, src, dst, device):
        slot = len(self.made)
        copy = pltpu.make_async_remote_copy(
            src_ref=src,
            dst_ref=dst,
            send_sem=self.send.at[slot],
            recv_sem=self.recv.at[slot],
            device_id=device,
            device_id_type=MESH,
        )
        copy.start()
        self.made[key] = copy

    def arrived(self, key):
        self.made[key].wait_recv()

    def finish(self):
        for copy in self.made.values():
            copy.wait_send()


def n_copies():
    return CHUNKS * (3 + 24 + 3 + 3) + 6 + 24 + 4 + 17 + 10 + 7


def step_kernel(
    act_hbm,
    grads,
    codes1_hbm,
    codes2_hbm,
    scales_hbm,
    rows_hbm,
    cols_hbm,
    update,
    first_normed,
    first_peaks,
    second,
    rinv_out,
    rp_out,
    cp_out,
    act,
    codes1,
    codes2,
    scales,
    rows,
    cols,
    at,
    bb,
    gs,
    gs_scale,
    gi,
    gi_scale,
    mom,
    acc,
    sq,
    ss_src,
    ss_dst,
    cp_a,
    cp_b,
    cp_dst,
    rp_a,
    rp_dst,
    rowacc,
    colacc,
    send,
    recv,
    local,
):
    r, c = lax.axis_index("row"), lax.axis_index("col")
    z, y = r // NY, r % NY
    x, k = c // 2, c % 2

    def to_z(d):
        return ((z + d + NZ) % NZ * NY + y, c)

    def to_y(d):
        return (z * NY + (y + d) % NY, c)

    def to_x(d):
        return (r, (x + d) % NX * 2 + k)

    peer = (r, x * 2 + 1 - k)
    near = [(d, to_x(d)) for d in (1, 3, 2)] + [
        (4 + d, (r, (x + d) % NX * 2 + 1 - k)) for d in (0, 1, 3, 2)
    ]

    barrier = pltpu.get_barrier_semaphore()
    partners = (
        [to_z(d) for d in range(1, NZ)]
        + [to_y(d) for d in (1, 3, 2)]
        + [device for _, device in near]
    )
    for partner in partners:
        pl.semaphore_signal(barrier, inc=1, device_id=partner, device_id_type=MESH)

    pairs = (
        (act_hbm, act),
        (codes2_hbm, codes2),
        (rows_hbm, rows),
        (cols_hbm, cols),
        (scales_hbm, scales),
        (codes1_hbm, codes1),
    )
    loads = [pltpu.make_async_copy(src, dst, local.at[i]) for i, (src, dst) in enumerate(pairs)]
    for load in loads:
        load.start()

    def place(way, distance):
        if distance == 4:
            return FAR
        return (distance if way < 0 or distance == 0 else 3 + distance) * ZROWS

    def tokens(cc):
        ahead = (cc - z + NZ) % NZ
        return pl.ds((ahead + ahead // 4 * (11 - 2 * ahead)) * ROWS, ROWS)

    def spot(yy, cc, half=None):
        if half is None:
            return at.at[pl.ds(yy * ROWS, ROWS), tokens(cc)]
        size = ROWS // 2
        return at.at[pl.ds(yy * ROWS + half * size, size), tokens(cc)]

    owns = []
    for n in range(CHUNKS):
        own = pltpu.make_async_copy(
            grads.at[:, pl.ds(y * PART + n * WIDTH, WIDTH)],
            bb.at[n, pl.ds(y * TOK, TOK)],
            local.at[len(pairs) + n],
        )
        own.start()
        owns.append(own)
    loads[0].wait()
    spot(y, c)[...] = act[...].T

    def decode_second():
        for load in loads[1:4]:
            load.wait()
        rowacc[...] = jnp.broadcast_to(rows[...].reshape(1, ROWS), (LANES, ROWS)).T * (0.95 / 16.0)

        @pl.loop(0, ROWS // TILE)
        def _(i):
            at_rows = pl.ds(pl.multiple_of(i * TILE, TILE), TILE)
            row = rowacc[at_rows, :]
            for b in range(BLOCKS):
                word = codes2[at_rows, pl.ds(b // 2 * LANES, LANES)]
                code = word & 15 if b % 2 == 0 else word >> 4
                col = cols[pl.ds(b * LANES, LANES)].reshape(1, LANES) * (0.95 / 16.0)
                second[b, at_rows, :] = jnp.minimum(row, col) * (code.astype(jnp.float32) + 1.0)

    def decode_first():
        for load in loads[4:]:
            load.wait()
        wide = jnp.concatenate(
            [scales[...], jnp.zeros((LANES - BLOCKS, ROWS), jnp.float32)], axis=0
        )
        rowacc[...] = wide.T * (0.9 / 7.5)

        @pl.loop(0, ROWS // TILE)
        def _(i):
            at_rows = pl.ds(pl.multiple_of(i * TILE, TILE), TILE)
            scale = rowacc[at_rows, :]
            for b in range(BLOCKS):
                word = codes1[at_rows, pl.ds(b // 2 * LANES, LANES)]
                code = word & 15 if b % 2 == 0 else word >> 4
                mom[b, at_rows, :] = scale[:, b : b + 1] * (code.astype(jnp.float32) - 7.5)

    pl.semaphore_wait(barrier, len(partners))

    net = Copies(send, recv)
    ring = (1, 3, 2)

    def spread(n):
        for d in ring:
            other = (y + d) % NY
            net.start(
                ("b1", n, d),
                grads.at[:, pl.ds(other * PART + n * WIDTH, WIDTH)],
                bb.at[n, pl.ds(y * TOK, TOK)],
                to_y(d),
            )

    def pass_on(n, s):
        if s == 1:
            owns[n].wait()
            for d in ring:
                net.arrived(("b1", n, d))
        for i in range(3):
            for way in (1, -1):
                if s > 1:
                    net.arrived(("b2", n, s - 1, way, i))
                for j in range(3):
                    if s < 4:
                        need, (first, size) = j, PIECES[j]
                    elif way > 0:
                        need, (first, size) = (0, 0, 1)[j], HALF_PIECES[j]
                    else:
                        need, (first, size) = (1, 2, 2)[j], HALF_PIECES[j]
                        first += ZROWS // 2
                    if need == i:
                        net.start(
                            ("b2", n, s, way, j),
                            bb.at[n, pl.ds(place(way, s - 1) + first, size)],
                            bb.at[n, pl.ds(place(way, s) + first, size)],
                            to_z(way),
                        )

    spread(0)
    for d in ring:
        ref = spot(y, c, 0)
        net.start(("ay", 0, d), ref, ref, to_y(d))
        ref = spot(y, c, 1)
        net.start(("ax", 0, d), ref, ref, to_x(d))
    for d in ring:
        ref = spot(y, c, 0)
        net.start(("axy", 0, d), ref, ref, to_x(d))
        ref = spot(y, c, 1)
        net.start(("ayx", 0, d), ref, ref, to_y(d))
    decode_second()
    pass_on(0, 1)
    for e in ring:
        net.arrived(("ay", 0, e))
        ref = spot((y + NY - e) % NY, c, 0)
        for d in ring:
            net.start(("axy", e, d), ref, ref, to_x(d))
        net.arrived(("ax", 0, e))
        ref = spot(y, (x + NX - e) % NX * 2 + k, 1)
        for d in ring:
            net.start(("ayx", e, d), ref, ref, to_y(d))
    spread(1)

    def to_peer(q):
        if q == 0:
            for d in ring:
                net.arrived(("ayx", 0, d))
        else:
            for e in (0,) + ring:
                net.arrived(("axy", e, q))
            for d in ring:
                net.arrived(("ayx", q, d))
        ref = at.at[:, tokens((x + NX - q) % NX * 2 + k)]
        net.start(("peer", q), ref, ref, peer)

    sq[...] = jnp.zeros_like(sq)

    order = (2, 1, 3, 0)

    def product(n, d, first, size):
        other = (y + d) % NY
        return jnp.dot(
            at[pl.ds(pl.multiple_of(other * ROWS, ROWS), ROWS), pl.ds(first, size)],
            bb[n, pl.ds(first, size)],
            preferred_element_type=jnp.float32,
        )

    def pack(n, d, res):
        tiles = res.reshape(ROWS // 8, 8, WIDTH)
        sq[...] += jnp.sum(tiles * tiles, axis=0)
        top = jnp.max(jnp.max(jnp.abs(tiles), axis=0), axis=0, keepdims=True)
        top = jnp.maximum(top, 1e-30)
        words = jnp.round(res * (32767.0 / top)).astype(jnp.int32).astype(jnp.int16)
        scale = jnp.broadcast_to(top * (1.0 / 32767.0), (8, WIDTH))
        block = y * (PART // LANES) + n * WB
        for w in range(WB):
            at_cols = slice(w * LANES, (w + 1) * LANES)
            if d:
                gs[n, d - 1, w] = words[:, at_cols]
                gs_scale[n, d - 1, w] = scale[:, at_cols]
            else:
                gi[block + w] = words[:, at_cols]
                gi_scale[block + w] = scale[:, at_cols]

    def hand_out(n, d):
        block = pl.ds(y * (PART // LANES) + n * WB, WB)
        net.start(("out", n, d), gs.at[n, d - 1], gi.at[block], to_y(d))
        net.start(("scale", n, d), gs_scale.at[n, d - 1], gi_scale.at[block], to_y(d))

    def far_arrived(n):
        for way in (1, -1):
            for j in range(3):
                net.arrived(("b2", n, 4, way, j))

    pass_on(0, 2)
    decode_first()
    pass_on(0, 3)
    pass_on(1, 1)
    pass_on(0, 4)
    pass_on(1, 2)
    for q in (0,) + ring:
        to_peer(q)
    pass_on(1, 3)
    for q in (0,) + ring:
        net.arrived(("peer", q))
    far_arrived(0)
    for d in order:
        pack(0, d, product(0, d, 0, TOKENS))
        if d:
            hand_out(0, d)
    pass_on(1, 4)
    for d in order:
        acc[d] = product(1, d, 0, FAR)
    far_arrived(1)
    for d in order:
        pack(1, d, acc[d] + product(1, d, FAR, ZROWS))

    ss_src[0] = jnp.full((8, LANES), jnp.sum(sq[...]))
    stages = [
        near,
        [(d, to_z(d)) for d in (4, 3, 5, 2, 6, 1, 7)],
        [(d, to_y(d)) for d in ring],
    ]
    slot = 0
    for i, stage in enumerate(stages):
        for j, (d, device) in enumerate(stage):
            net.start(("ss", i, d), ss_src.at[i], ss_dst.at[slot + j], device)
        if i == 0:
            for d in ring:
                hand_out(1, d)
        total = ss_src[i]
        for j, (d, device) in enumerate(stage):
            net.arrived(("ss", i, d))
            total = total + ss_dst[slot + j]
        slot += len(stage)
        if i < 2:
            ss_src[i + 1] = total
    limit = float(D) * FF
    clip = jnp.where(total <= limit, 1.0, jnp.sqrt(limit / jnp.maximum(total, limit)))

    for n in range(CHUNKS):
        for d in ring:
            net.arrived(("out", n, d))
            net.arrived(("scale", n, d))

    rate = clip[0:1, :]
    colacc[...] = jnp.zeros_like(colacc)

    @pl.loop(0, ROWS // TILE)
    def _(i):
        at_rows = pl.ds(pl.multiple_of(i * TILE, TILE), TILE)
        best = jnp.zeros((TILE, LANES), jnp.float32)
        for b in range(BLOCKS):
            words = gi[b, at_rows, :].astype(jnp.int32).astype(jnp.float32)
            scaled = words * (gi_scale[b, 0:1, :] * rate)
            value = second[b, at_rows, :] + 0.05 * scaled * scaled
            second[b, at_rows, :] = value
            mom[b, at_rows, :] += 0.1 * scaled
            best = jnp.maximum(best, value)
            colacc[b] = jnp.maximum(colacc[b], jnp.max(value.reshape(TILE // 8, 8, LANES), axis=0))
        rowacc[at_rows, :] = best

    for b in range(BLOCKS):
        cp_a[b : b + 1, :] = jnp.max(colacc[b], axis=0, keepdims=True)
    for j, d in enumerate(ring):
        net.start(("cy", d), cp_a, cp_dst.at[j], to_y(d))
    rp_a[...] = jnp.broadcast_to(jnp.max(rowacc[...].T, axis=0, keepdims=True), (8, ROWS))
    for j, (d, device) in enumerate(near):
        net.start(("rx", d), rp_a, rp_dst.at[j], device)

    def advance(first, last):
        lane = lax.broadcasted_iota(jnp.int32, (TILE, LANES), 1)

        @pl.loop(first, last)
        def _(i):
            at_rows = pl.ds(pl.multiple_of(i * TILE, TILE), TILE)
            peaks = jnp.zeros((TILE, LANES), jnp.float32)
            for b in range(BLOCKS):
                at_cols = pl.ds(b * LANES, LANES)
                value = mom[b, at_rows, :]
                peak = jnp.max(jnp.abs(value), axis=1, keepdims=True)
                peaks = jnp.where(lane == b, peak, peaks)
                first_normed[at_rows, at_cols] = (value * inverse(peak + 1e-06)).astype(
                    jnp.bfloat16
                )
                under = second[b, at_rows, :] * (1.0 / BIAS_TWO)
                root = under * lax.rsqrt(under) + 1e-08
                update[at_rows, at_cols] = (value * (1.0 / BIAS_ONE)) * inverse(root)
            rowacc[at_rows, :] = peaks

    advance(0, 3)
    for d in ring:
        net.arrived(("cy", d))
    cp_b[...] = jnp.maximum(
        jnp.maximum(cp_a[...], cp_dst[0]), jnp.maximum(cp_dst[1], cp_dst[2])
    )
    for d in (4, 3, 5, 2, 6, 1, 7):
        net.start(("cz", d), cp_b, cp_dst.at[2 + d], to_z(d))
    advance(3, ROWS // TILE)
    first_peaks[...] = rowacc[...].T[:BLOCKS, :]
    peaks = rp_a[...]
    for j, (d, _) in enumerate(near):
        net.arrived(("rx", d))
        peaks = jnp.maximum(peaks, rp_dst[j])
    rp_out[...] = peaks
    rinv_out[...] = jnp.broadcast_to((1.0 / peaks)[0:1, :], (LANES, ROWS)).T
    tops = cp_b[...]
    for d in range(1, NZ):
        net.arrived(("cz", d))
        tops = jnp.maximum(tops, cp_dst[2 + d])
    cp_out[...] = tops
    net.finish()


def inverse(value):
    guess = pltpu.reciprocal(value, approx=True)
    return guess * (2.0 - value * guess)


def finish_kernel(
    update_in,
    first_in,
    peaks_in,
    second,
    rinv,
    rp,
    cp,
    update,
    first_normed,
    first_peaks,
    second_normed,
    row_peaks,
    col_peaks,
    normed,
    sems,
):
    copies = [
        pltpu.make_async_copy(update_in, update, sems.at[0]),
        pltpu.make_async_copy(first_in, first_normed, sems.at[1]),
        pltpu.make_async_copy(peaks_in, first_peaks, sems.at[2]),
    ]
    for copy in copies:
        copy.start()
    row_peaks[...] = rp[0:1, :].reshape(ROWS)
    for b in range(BLOCKS):
        col_peaks[pl.ds(b * LANES, LANES)] = cp[b : b + 1, :].reshape(LANES)
    cinv = 1.0 / cp[...]
    for i in range(ROWS // FINISH):
        at_rows = pl.ds(i * FINISH, FINISH)
        for b in range(BLOCKS):
            normed[at_rows, pl.ds(b * LANES, LANES)] = (
                second[b, at_rows, :] * jnp.maximum(rinv[at_rows, :], cinv[b : b + 1, :])
            ).astype(jnp.bfloat16)
        copy = pltpu.make_async_copy(
            normed.at[at_rows], second_normed.at[at_rows], sems.at[3 + i]
        )
        copy.start()
        copies.append(copy)
    for copy in copies:
        copy.wait()


def local(activations, output_grads, first_codes, second_codes, first_scales, second_rows, second_cols):
    f32, bf16 = jnp.float32, jnp.bfloat16
    vmem = pl.BlockSpec(memory_space=pltpu.VMEM)
    hbm = pl.BlockSpec(memory_space=pltpu.HBM)
    update, first_normed, first_peaks, second, rinv, rp, cp = pl.pallas_call(
        step_kernel,
        out_shape=(
            jax.ShapeDtypeStruct((ROWS, COLS), f32),
            jax.ShapeDtypeStruct((ROWS, COLS), bf16),
            jax.ShapeDtypeStruct((BLOCKS, ROWS), f32),
            jax.ShapeDtypeStruct((BLOCKS, ROWS, LANES), f32),
            jax.ShapeDtypeStruct((ROWS, LANES), f32),
            jax.ShapeDtypeStruct((8, ROWS), f32),
            jax.ShapeDtypeStruct((BLOCKS, LANES), f32),
        ),
        in_specs=[hbm] * 7,
        out_specs=(vmem,) * 7,
        scratch_shapes=[
            pltpu.VMEM((ROWS, ROWS), bf16),
            pltpu.VMEM((ROWS, COLS // 2), jnp.int32),
            pltpu.VMEM((ROWS, COLS // 2), jnp.int32),
            pltpu.VMEM((BLOCKS, ROWS), f32),
            pltpu.VMEM((ROWS,), f32),
            pltpu.VMEM((COLS,), f32),
            pltpu.VMEM((NY * ROWS, TOKENS), bf16),
            pltpu.VMEM((CHUNKS, TOKENS, WIDTH), bf16),
            pltpu.VMEM((CHUNKS, 3, WB, ROWS, LANES), jnp.int16),
            pltpu.VMEM((CHUNKS, 3, WB, 8, LANES), f32),
            pltpu.VMEM((BLOCKS, ROWS, LANES), jnp.int16),
            pltpu.VMEM((BLOCKS, 8, LANES), f32),
            pltpu.VMEM((BLOCKS, ROWS, LANES), f32),
            pltpu.VMEM((NY, ROWS, WIDTH), f32),
            pltpu.VMEM((8, WIDTH), f32),
            pltpu.VMEM((3, 8, LANES), f32),
            pltpu.VMEM((17, 8, LANES), f32),
            pltpu.VMEM((BLOCKS, LANES), f32),
            pltpu.VMEM((BLOCKS, LANES), f32),
            pltpu.VMEM((10, BLOCKS, LANES), f32),
            pltpu.VMEM((8, ROWS), f32),
            pltpu.VMEM((7, 8, ROWS), f32),
            pltpu.VMEM((ROWS, LANES), f32),
            pltpu.VMEM((BLOCKS, 8, LANES), f32),
            pltpu.SemaphoreType.DMA((n_copies(),)),
            pltpu.SemaphoreType.DMA((n_copies(),)),
            pltpu.SemaphoreType.DMA((6 + CHUNKS,)),
        ],
        compiler_params=pltpu.CompilerParams(
            collective_id=0, has_side_effects=True, vmem_limit_bytes=40 * 2**20
        ),
        name="step",
    )(
        *(
            pltpu.with_memory_space_constraint(array, pltpu.HBM)
            for array in (
                activations,
                output_grads,
                first_codes,
                second_codes,
                first_scales.T,
                second_rows,
                second_cols,
            )
        )
    )
    update, first_normed, first_peaks, second_normed, row_peaks, col_peaks = pl.pallas_call(
        finish_kernel,
        out_shape=(
            jax.ShapeDtypeStruct((ROWS, COLS), f32),
            jax.ShapeDtypeStruct((ROWS, COLS), bf16),
            jax.ShapeDtypeStruct((BLOCKS, ROWS), f32),
            jax.ShapeDtypeStruct((ROWS, COLS), bf16),
            jax.ShapeDtypeStruct((ROWS,), f32),
            jax.ShapeDtypeStruct((COLS,), f32),
        ),
        in_specs=[vmem] * 7,
        out_specs=(hbm, hbm, hbm, hbm, vmem, vmem),
        scratch_shapes=[
            pltpu.VMEM((ROWS, COLS), bf16),
            pltpu.SemaphoreType.DMA((3 + ROWS // FINISH,)),
        ],
        compiler_params=pltpu.CompilerParams(vmem_limit_bytes=16 * 2**20),
        name="finish",
    )(update, first_normed, first_peaks, second, rinv, rp, cp)
    return update, first_normed, first_peaks.T, second_normed, row_peaks, col_peaks


def solution(mesh):
    return jax.shard_map(
        local,
        mesh=mesh,
        in_specs=(
            P("col", "row"),
            P("row", "col"),
            P("row", "col"),
            P("row", "col"),
            P("row", "col"),
            P("row"),
            P("col"),
        ),
        out_specs=(
            P("row", "col"),
            P("row", "col"),
            P("row", "col"),
            P("row", "col"),
            P("row"),
            P("col"),
        ),
        check_vma=False,
    )
```

```python
import jax
import jax.numpy as jnp
from jax import lax
from jax.experimental import pallas as pl
from jax.experimental.pallas import tpu as pltpu
from jax.sharding import PartitionSpec as P

MESH = pl.DeviceIdType.MESH
D = 8192
FF = 24576
TOKENS = 2048
ROWS = 256
COLS = 3072
NZ, NY, NX = 8, 4, 4
PART = COLS // NY
CHUNKS = 2
WIDTH = PART // CHUNKS
LANES = 128
WB = WIDTH // LANES
TILE = 32
FINISH = 64
BLOCKS = COLS // LANES
ZROWS = TOKENS // NZ
FAR = TOKENS - ZROWS
SPLIT = (192, 64)
TOK = TOKENS // (NZ * NY)

BIAS_ONE = 1.0 - 0.9**10
BIAS_TWO = 1.0 - 0.95**10


class Copies:
    def __init__(self, send, recv):
        self.send, self.recv = send, recv
        self.made = {}

    def start(self, key, src, dst, device):
        slot = len(self.made)
        copy = pltpu.make_async_remote_copy(
            src_ref=src,
            dst_ref=dst,
            send_sem=self.send.at[slot],
            recv_sem=self.recv.at[slot],
            device_id=device,
            device_id_type=MESH,
        )
        copy.start()
        self.made[key] = copy

    def arrived(self, key):
        self.made[key].wait_recv()

    def finish(self):
        for copy in self.made.values():
            copy.wait_send()


def n_copies():
    return CHUNKS * (3 + 28 + 3 + 3) + 6 + 24 + 4 + 17 + 10 + 7


def step_kernel(
    act_hbm,
    grads,
    codes1_hbm,
    codes2_hbm,
    scales_hbm,
    rows_hbm,
    cols_hbm,
    update,
    first_normed,
    first_peaks,
    second,
    rinv_out,
    rp_out,
    cp_out,
    act,
    codes1,
    codes2,
    scales,
    rows,
    cols,
    at,
    bb,
    gs,
    gs_scale,
    gi,
    gi_scale,
    mom,
    acc,
    sq,
    ss_src,
    ss_dst,
    cp_a,
    cp_b,
    cp_dst,
    rp_a,
    rp_dst,
    rowacc,
    colacc,
    send,
    recv,
    local,
):
    r, c = lax.axis_index("row"), lax.axis_index("col")
    z, y = r // NY, r % NY
    x, k = c // 2, c % 2

    def to_z(d):
        return ((z + d + NZ) % NZ * NY + y, c)

    def to_y(d):
        return (z * NY + (y + d) % NY, c)

    def to_x(d):
        return (r, (x + d) % NX * 2 + k)

    peer = (r, x * 2 + 1 - k)
    near = [(d, to_x(d)) for d in (1, 3, 2)] + [
        (4 + d, (r, (x + d) % NX * 2 + 1 - k)) for d in (0, 1, 3, 2)
    ]

    barrier = pltpu.get_barrier_semaphore()
    partners = (
        [to_z(d) for d in (1, 7)]
        + [to_y(d) for d in (1, 3, 2)]
        + [device for _, device in near]
    )
    for partner in partners:
        pl.semaphore_signal(barrier, inc=1, device_id=partner, device_id_type=MESH)

    pairs = (
        (act_hbm, act),
        (codes2_hbm, codes2),
        (rows_hbm, rows),
        (cols_hbm, cols),
        (scales_hbm, scales),
        (codes1_hbm, codes1),
    )
    loads = [pltpu.make_async_copy(src, dst, local.at[i]) for i, (src, dst) in enumerate(pairs)]
    for load in loads:
        load.start()

    def place(way, distance):
        if distance == 4:
            return FAR
        return (distance if way < 0 or distance == 0 else 3 + distance) * ZROWS

    def tokens(cc):
        ahead = (cc - z + NZ) % NZ
        return pl.ds((ahead + ahead // 4 * (11 - 2 * ahead)) * ROWS, ROWS)

    def spot(yy, cc, half=None):
        if half is None:
            return at.at[pl.ds(yy * ROWS, ROWS), tokens(cc)]
        return at.at[pl.ds(yy * ROWS + half * SPLIT[0], SPLIT[half]), tokens(cc)]

    owns = []
    for n in range(CHUNKS):
        own = pltpu.make_async_copy(
            grads.at[:, pl.ds(y * PART + n * WIDTH, WIDTH)],
            bb.at[n, pl.ds(y * TOK, TOK)],
            local.at[len(pairs) + n],
        )
        own.start()
        owns.append(own)
    loads[0].wait()
    spot(y, c)[...] = act[...].T

    def decode_second():
        for load in loads[1:4]:
            load.wait()
        rowacc[...] = jnp.broadcast_to(rows[...].reshape(1, ROWS), (LANES, ROWS)).T * (0.95 / 16.0)

        @pl.loop(0, ROWS // TILE)
        def _(i):
            at_rows = pl.ds(pl.multiple_of(i * TILE, TILE), TILE)
            row = rowacc[at_rows, :]
            for b in range(BLOCKS):
                word = codes2[at_rows, pl.ds(b // 2 * LANES, LANES)]
                code = word & 15 if b % 2 == 0 else word >> 4
                col = cols[pl.ds(b * LANES, LANES)].reshape(1, LANES) * (0.95 / 16.0)
                second[b, at_rows, :] = jnp.minimum(row, col) * (code.astype(jnp.float32) + 1.0)

    def decode_first():
        for load in loads[4:]:
            load.wait()
        wide = jnp.concatenate(
            [scales[...], jnp.zeros((LANES - BLOCKS, ROWS), jnp.float32)], axis=0
        )
        rowacc[...] = wide.T * (0.9 / 7.5)

        @pl.loop(0, ROWS // TILE)
        def _(i):
            at_rows = pl.ds(pl.multiple_of(i * TILE, TILE), TILE)
            scale = rowacc[at_rows, :]
            for b in range(BLOCKS):
                word = codes1[at_rows, pl.ds(b // 2 * LANES, LANES)]
                code = word & 15 if b % 2 == 0 else word >> 4
                mom[b, at_rows, :] = scale[:, b : b + 1] * (code.astype(jnp.float32) - 7.5)

    pl.semaphore_wait(barrier, len(partners))

    net = Copies(send, recv)
    ring = (1, 3, 2)

    def spread(n):
        for d in ring:
            other = (y + d) % NY
            net.start(
                ("b1", n, d),
                grads.at[:, pl.ds(other * PART + n * WIDTH, WIDTH)],
                bb.at[n, pl.ds(y * TOK, TOK)],
                to_y(d),
            )

    def pass_on(n, s, pieces=(0, 1, 2, 3)):
        for i in pieces:
            d = ((0,) + ring)[i]
            if s == 1 and d:
                net.arrived(("b1", n, d))
            elif s == 1:
                owns[n].wait()
            first = (y - d + NY) % NY * TOK
            for way in (1, -1):
                if s > 1:
                    net.arrived(("b2", n, s - 1, way, i))
                if s < 4 or (way > 0) == (i < 2):
                    net.start(
                        ("b2", n, s, way, i),
                        bb.at[n, pl.ds(place(way, s - 1) + first, TOK)],
                        bb.at[n, pl.ds(place(way, s) + first, TOK)],
                        to_z(way),
                    )

    pass_on(0, 1, (0,))
    spread(0)
    for d in ring:
        ref = spot(y, c, 0)
        net.start(("ay", 0, d), ref, ref, to_y(d))
        ref = spot(y, c, 1)
        net.start(("ax", 0, d), ref, ref, to_x(d))
    for d in ring:
        ref = spot(y, c, 0)
        net.start(("axy", 0, d), ref, ref, to_x(d))
        ref = spot(y, c, 1)
        net.start(("ayx", 0, d), ref, ref, to_y(d))
    pass_on(0, 1, (1, 2, 3))
    for e in ring:
        net.arrived(("ay", 0, e))
        ref = spot((y + NY - e) % NY, c, 0)
        for d in ring:
            net.start(("axy", e, d), ref, ref, to_x(d))
        net.arrived(("ax", 0, e))
        ref = spot(y, (x + NX - e) % NX * 2 + k, 1)
        for d in ring:
            net.start(("ayx", e, d), ref, ref, to_y(d))
    spread(1)

    def to_peer(q):
        if q == 0:
            for d in ring:
                net.arrived(("ayx", 0, d))
        else:
            for e in (0,) + ring:
                net.arrived(("axy", e, q))
            for d in ring:
                net.arrived(("ayx", q, d))
        ref = at.at[:, tokens((x + NX - q) % NX * 2 + k)]
        net.start(("peer", q), ref, ref, peer)

    sq[...] = jnp.zeros_like(sq)

    order = (2, 1, 3, 0)

    def product(n, d, first, size):
        other = (y + d) % NY
        return jnp.dot(
            at[pl.ds(pl.multiple_of(other * ROWS, ROWS), ROWS), pl.ds(first, size)],
            bb[n, pl.ds(first, size)],
            preferred_element_type=jnp.float32,
        )

    def pack(n, d, res):
        tiles = res.reshape(ROWS // 8, 8, WIDTH)
        sq[...] += jnp.sum(tiles * tiles, axis=0)
        top = jnp.max(jnp.max(jnp.abs(tiles), axis=0), axis=0, keepdims=True)
        top = jnp.maximum(top, 1e-30)
        words = jnp.round(res * (32767.0 / top)).astype(jnp.int32).astype(jnp.int16)
        scale = jnp.broadcast_to(top * (1.0 / 32767.0), (8, WIDTH))
        block = y * (PART // LANES) + n * WB
        for w in range(WB):
            at_cols = slice(w * LANES, (w + 1) * LANES)
            if d:
                gs[n, d - 1, w] = words[:, at_cols]
                gs_scale[n, d - 1, w] = scale[:, at_cols]
            else:
                gi[block + w] = words[:, at_cols]
                gi_scale[block + w] = scale[:, at_cols]

    def hand_out(n, d):
        block = pl.ds(y * (PART // LANES) + n * WB, WB)
        net.start(("out", n, d), gs.at[n, d - 1], gi.at[block], to_y(d))
        net.start(("scale", n, d), gs_scale.at[n, d - 1], gi_scale.at[block], to_y(d))

    def far_arrived(n):
        for i in range(NY):
            net.arrived(("b2", n, 4, 1 if i < 2 else -1, i))

    pass_on(0, 2)
    decode_second()
    pass_on(0, 3)
    pass_on(1, 1)
    decode_first()
    pass_on(0, 4)
    pass_on(1, 2)
    for q in (0,) + ring:
        to_peer(q)
    pass_on(1, 3)
    for q in (0,) + ring:
        net.arrived(("peer", q))
    far_arrived(0)
    for d in order:
        pack(0, d, product(0, d, 0, TOKENS))
        if d:
            hand_out(0, d)
    pass_on(1, 4)
    for d in order:
        acc[d] = product(1, d, 0, FAR)
    far_arrived(1)
    for d in order:
        pack(1, d, acc[d] + product(1, d, FAR, ZROWS))

    ss_src[0] = jnp.full((8, LANES), jnp.sum(sq[...]))
    stages = [
        near,
        [(d, to_z(d)) for d in (4, 3, 5, 2, 6, 1, 7)],
        [(d, to_y(d)) for d in ring],
    ]
    slot = 0
    for i, stage in enumerate(stages):
        for j, (d, device) in enumerate(stage):
            net.start(("ss", i, d), ss_src.at[i], ss_dst.at[slot + j], device)
        if i == 0:
            for d in ring:
                hand_out(1, d)
        total = ss_src[i]
        for j, (d, device) in enumerate(stage):
            net.arrived(("ss", i, d))
            total = total + ss_dst[slot + j]
        slot += len(stage)
        if i < 2:
            ss_src[i + 1] = total
    limit = float(D) * FF
    clip = jnp.where(total <= limit, 1.0, jnp.sqrt(limit / jnp.maximum(total, limit)))

    for n in range(CHUNKS):
        for d in ring:
            net.arrived(("out", n, d))
            net.arrived(("scale", n, d))

    rate = clip[0:1, :]
    colacc[...] = jnp.zeros_like(colacc)

    @pl.loop(0, ROWS // TILE)
    def _(i):
        at_rows = pl.ds(pl.multiple_of(i * TILE, TILE), TILE)
        best = jnp.zeros((TILE, LANES), jnp.float32)
        for b in range(BLOCKS):
            words = gi[b, at_rows, :].astype(jnp.int32).astype(jnp.float32)
            scaled = words * (gi_scale[b, 0:1, :] * rate)
            value = second[b, at_rows, :] + 0.05 * scaled * scaled
            second[b, at_rows, :] = value
            mom[b, at_rows, :] += 0.1 * scaled
            best = jnp.maximum(best, value)
            colacc[b] = jnp.maximum(colacc[b], jnp.max(value.reshape(TILE // 8, 8, LANES), axis=0))
        rowacc[at_rows, :] = best

    for b in range(BLOCKS):
        cp_a[b : b + 1, :] = jnp.max(colacc[b], axis=0, keepdims=True)
    for j, d in enumerate(ring):
        net.start(("cy", d), cp_a, cp_dst.at[j], to_y(d))
    rp_a[...] = jnp.broadcast_to(jnp.max(rowacc[...].T, axis=0, keepdims=True), (8, ROWS))
    for j, (d, device) in enumerate(near):
        net.start(("rx", d), rp_a, rp_dst.at[j], device)

    def advance(first, last):
        lane = lax.broadcasted_iota(jnp.int32, (TILE, LANES), 1)

        @pl.loop(first, last)
        def _(i):
            at_rows = pl.ds(pl.multiple_of(i * TILE, TILE), TILE)
            peaks = jnp.zeros((TILE, LANES), jnp.float32)
            for b in range(BLOCKS):
                at_cols = pl.ds(b * LANES, LANES)
                value = mom[b, at_rows, :]
                peak = jnp.max(jnp.abs(value), axis=1, keepdims=True)
                peaks = jnp.where(lane == b, peak, peaks)
                first_normed[at_rows, at_cols] = (value * inverse(peak + 1e-06)).astype(
                    jnp.bfloat16
                )
                under = second[b, at_rows, :] * (1.0 / BIAS_TWO)
                root = under * lax.rsqrt(under) + 1e-08
                update[at_rows, at_cols] = (value * (1.0 / BIAS_ONE)) * inverse(root)
            rowacc[at_rows, :] = peaks

    advance(0, 3)
    for d in ring:
        net.arrived(("cy", d))
    cp_b[...] = jnp.maximum(
        jnp.maximum(cp_a[...], cp_dst[0]), jnp.maximum(cp_dst[1], cp_dst[2])
    )
    for d in (4, 3, 5, 2, 6, 1, 7):
        net.start(("cz", d), cp_b, cp_dst.at[2 + d], to_z(d))
    advance(3, ROWS // TILE)
    first_peaks[...] = rowacc[...].T[:BLOCKS, :]
    peaks = rp_a[...]
    for j, (d, _) in enumerate(near):
        net.arrived(("rx", d))
        peaks = jnp.maximum(peaks, rp_dst[j])
    rp_out[...] = peaks
    rinv_out[...] = jnp.broadcast_to((1.0 / peaks)[0:1, :], (LANES, ROWS)).T
    tops = cp_b[...]
    for d in range(1, NZ):
        net.arrived(("cz", d))
        tops = jnp.maximum(tops, cp_dst[2 + d])
    cp_out[...] = tops
    net.finish()


def inverse(value):
    guess = pltpu.reciprocal(value, approx=True)
    return guess * (2.0 - value * guess)


def finish_kernel(
    update_in,
    first_in,
    peaks_in,
    second,
    rinv,
    rp,
    cp,
    update,
    first_normed,
    first_peaks,
    second_normed,
    row_peaks,
    col_peaks,
    normed,
    sems,
):
    copies = [
        pltpu.make_async_copy(update_in, update, sems.at[0]),
        pltpu.make_async_copy(first_in, first_normed, sems.at[1]),
        pltpu.make_async_copy(peaks_in, first_peaks, sems.at[2]),
    ]
    for copy in copies:
        copy.start()
    row_peaks[...] = rp[0:1, :].reshape(ROWS)
    for b in range(BLOCKS):
        col_peaks[pl.ds(b * LANES, LANES)] = cp[b : b + 1, :].reshape(LANES)
    cinv = 1.0 / cp[...]
    for i in range(ROWS // FINISH):
        at_rows = pl.ds(i * FINISH, FINISH)
        for b in range(BLOCKS):
            normed[at_rows, pl.ds(b * LANES, LANES)] = (
                second[b, at_rows, :] * jnp.maximum(rinv[at_rows, :], cinv[b : b + 1, :])
            ).astype(jnp.bfloat16)
        copy = pltpu.make_async_copy(
            normed.at[at_rows], second_normed.at[at_rows], sems.at[3 + i]
        )
        copy.start()
        copies.append(copy)
    for copy in copies:
        copy.wait()


def local(activations, output_grads, first_codes, second_codes, first_scales, second_rows, second_cols):
    f32, bf16 = jnp.float32, jnp.bfloat16
    vmem = pl.BlockSpec(memory_space=pltpu.VMEM)
    hbm = pl.BlockSpec(memory_space=pltpu.HBM)
    update, first_normed, first_peaks, second, rinv, rp, cp = pl.pallas_call(
        step_kernel,
        out_shape=(
            jax.ShapeDtypeStruct((ROWS, COLS), f32),
            jax.ShapeDtypeStruct((ROWS, COLS), bf16),
            jax.ShapeDtypeStruct((BLOCKS, ROWS), f32),
            jax.ShapeDtypeStruct((BLOCKS, ROWS, LANES), f32),
            jax.ShapeDtypeStruct((ROWS, LANES), f32),
            jax.ShapeDtypeStruct((8, ROWS), f32),
            jax.ShapeDtypeStruct((BLOCKS, LANES), f32),
        ),
        in_specs=[hbm] * 7,
        out_specs=(vmem,) * 7,
        scratch_shapes=[
            pltpu.VMEM((ROWS, ROWS), bf16),
            pltpu.VMEM((ROWS, COLS // 2), jnp.int32),
            pltpu.VMEM((ROWS, COLS // 2), jnp.int32),
            pltpu.VMEM((BLOCKS, ROWS), f32),
            pltpu.VMEM((ROWS,), f32),
            pltpu.VMEM((COLS,), f32),
            pltpu.VMEM((NY * ROWS, TOKENS), bf16),
            pltpu.VMEM((CHUNKS, TOKENS, WIDTH), bf16),
            pltpu.VMEM((CHUNKS, 3, WB, ROWS, LANES), jnp.int16),
            pltpu.VMEM((CHUNKS, 3, WB, 8, LANES), f32),
            pltpu.VMEM((BLOCKS, ROWS, LANES), jnp.int16),
            pltpu.VMEM((BLOCKS, 8, LANES), f32),
            pltpu.VMEM((BLOCKS, ROWS, LANES), f32),
            pltpu.VMEM((NY, ROWS, WIDTH), f32),
            pltpu.VMEM((8, WIDTH), f32),
            pltpu.VMEM((3, 8, LANES), f32),
            pltpu.VMEM((17, 8, LANES), f32),
            pltpu.VMEM((BLOCKS, LANES), f32),
            pltpu.VMEM((BLOCKS, LANES), f32),
            pltpu.VMEM((10, BLOCKS, LANES), f32),
            pltpu.VMEM((8, ROWS), f32),
            pltpu.VMEM((7, 8, ROWS), f32),
            pltpu.VMEM((ROWS, LANES), f32),
            pltpu.VMEM((BLOCKS, 8, LANES), f32),
            pltpu.SemaphoreType.DMA((n_copies(),)),
            pltpu.SemaphoreType.DMA((n_copies(),)),
            pltpu.SemaphoreType.DMA((6 + CHUNKS,)),
        ],
        compiler_params=pltpu.CompilerParams(
            collective_id=0, has_side_effects=True, vmem_limit_bytes=40 * 2**20
        ),
        name="step",
    )(
        *(
            pltpu.with_memory_space_constraint(array, pltpu.HBM)
            for array in (
                activations,
                output_grads,
                first_codes,
                second_codes,
                first_scales.T,
                second_rows,
                second_cols,
            )
        )
    )
    update, first_normed, first_peaks, second_normed, row_peaks, col_peaks = pl.pallas_call(
        finish_kernel,
        out_shape=(
            jax.ShapeDtypeStruct((ROWS, COLS), f32),
            jax.ShapeDtypeStruct((ROWS, COLS), bf16),
            jax.ShapeDtypeStruct((BLOCKS, ROWS), f32),
            jax.ShapeDtypeStruct((ROWS, COLS), bf16),
            jax.ShapeDtypeStruct((ROWS,), f32),
            jax.ShapeDtypeStruct((COLS,), f32),
        ),
        in_specs=[vmem] * 7,
        out_specs=(hbm, hbm, hbm, hbm, vmem, vmem),
        scratch_shapes=[
            pltpu.VMEM((ROWS, COLS), bf16),
            pltpu.SemaphoreType.DMA((3 + ROWS // FINISH,)),
        ],
        compiler_params=pltpu.CompilerParams(vmem_limit_bytes=16 * 2**20),
        name="finish",
    )(update, first_normed, first_peaks, second, rinv, rp, cp)
    return update, first_normed, first_peaks.T, second_normed, row_peaks, col_peaks


def solution(mesh):
    return jax.shard_map(
        local,
        mesh=mesh,
        in_specs=(
            P("col", "row"),
            P("row", "col"),
            P("row", "col"),
            P("row", "col"),
            P("row", "col"),
            P("row"),
            P("col"),
        ),
        out_specs=(
            P("row", "col"),
            P("row", "col"),
            P("row", "col"),
            P("row", "col"),
            P("row"),
            P("col"),
        ),
        check_vma=False,
    )
```

```python
import jax
import jax.numpy as jnp
from jax import lax
from jax.experimental import pallas as pl
from jax.experimental.pallas import tpu as pltpu
from jax.sharding import PartitionSpec as P

MESH = pl.DeviceIdType.MESH
D = 8192
FF = 24576
TOKENS = 2048
ROWS = 256
COLS = 3072
NZ, NY, NX = 8, 4, 4
PART = COLS // NY
CHUNKS = 2
WIDTH = PART // CHUNKS
LANES = 128
WB = WIDTH // LANES
TILE = 32
FINISH = 64
BLOCKS = COLS // LANES
ZROWS = TOKENS // NZ
FAR = TOKENS - ZROWS
SPLIT = (192, 64)
TOK = TOKENS // (NZ * NY)

BIAS_ONE = 1.0 - 0.9**10
BIAS_TWO = 1.0 - 0.95**10


class Copies:
    def __init__(self, send, recv):
        self.send, self.recv = send, recv
        self.made = {}

    def start(self, key, src, dst, device):
        slot = len(self.made)
        copy = pltpu.make_async_remote_copy(
            src_ref=src,
            dst_ref=dst,
            send_sem=self.send.at[slot],
            recv_sem=self.recv.at[slot],
            device_id=device,
            device_id_type=MESH,
        )
        copy.start()
        self.made[key] = copy

    def arrived(self, key):
        self.made[key].wait_recv()

    def finish(self):
        for copy in self.made.values():
            copy.wait_send()


def n_copies():
    return CHUNKS * (3 + 28 + 3 + 3) + 6 + 24 + 4 + 17 + 10 + 7


def step_kernel(
    act_hbm,
    grads,
    codes1_hbm,
    codes2_hbm,
    scales_hbm,
    rows_hbm,
    cols_hbm,
    update,
    first_normed,
    first_peaks,
    second,
    rinv_out,
    rp_out,
    cp_out,
    act,
    codes1,
    codes2,
    scales,
    rows,
    cols,
    at,
    bb,
    gs,
    gs_scale,
    gi,
    gi_scale,
    mom,
    acc,
    sq,
    ss_src,
    ss_dst,
    cp_a,
    cp_b,
    cp_dst,
    rp_a,
    rp_dst,
    rowacc,
    colacc,
    send,
    recv,
    local,
):
    r, c = lax.axis_index("row"), lax.axis_index("col")
    z, y = r // NY, r % NY
    x, k = c // 2, c % 2

    def to_z(d):
        return ((z + d + NZ) % NZ * NY + y, c)

    def to_y(d):
        return (z * NY + (y + d) % NY, c)

    def to_x(d):
        return (r, (x + d) % NX * 2 + k)

    peer = (r, x * 2 + 1 - k)
    near = [(d, to_x(d)) for d in (1, 3, 2)] + [
        (4 + d, (r, (x + d) % NX * 2 + 1 - k)) for d in (0, 1, 3, 2)
    ]

    barrier = pltpu.get_barrier_semaphore()
    partners = (
        [to_z(d) for d in (1, 7)]
        + [to_y(d) for d in (1, 3, 2)]
        + [device for d, device in near if d <= 4]
    )
    for partner in partners:
        pl.semaphore_signal(barrier, inc=1, device_id=partner, device_id_type=MESH)

    pairs = (
        (act_hbm, act),
        (codes2_hbm, codes2),
        (rows_hbm, rows),
        (cols_hbm, cols),
        (scales_hbm, scales),
        (codes1_hbm, codes1),
    )
    loads = [pltpu.make_async_copy(src, dst, local.at[i]) for i, (src, dst) in enumerate(pairs)]
    for load in loads:
        load.start()

    def place(way, distance):
        if distance == 4:
            return FAR
        return (distance if way < 0 or distance == 0 else 3 + distance) * ZROWS

    def tokens(cc):
        ahead = (cc - z + NZ) % NZ
        return pl.ds((ahead + ahead // 4 * (11 - 2 * ahead)) * ROWS, ROWS)

    def spot(yy, cc, half=None):
        if half is None:
            return at.at[pl.ds(yy * ROWS, ROWS), tokens(cc)]
        return at.at[pl.ds(yy * ROWS + half * SPLIT[0], SPLIT[half]), tokens(cc)]

    owns = []
    for n in range(CHUNKS):
        own = pltpu.make_async_copy(
            grads.at[:, pl.ds(y * PART + n * WIDTH, WIDTH)],
            bb.at[n, pl.ds(y * TOK, TOK)],
            local.at[len(pairs) + n],
        )
        own.start()
        owns.append(own)
    loads[0].wait()
    spot(y, c)[...] = act[...].T

    def decode_second():
        for load in loads[1:4]:
            load.wait()
        rowacc[...] = jnp.broadcast_to(rows[...].reshape(1, ROWS), (LANES, ROWS)).T * (0.95 / 16.0)

        @pl.loop(0, ROWS // TILE)
        def _(i):
            at_rows = pl.ds(pl.multiple_of(i * TILE, TILE), TILE)
            row = rowacc[at_rows, :]
            for b in range(BLOCKS):
                word = codes2[at_rows, pl.ds(b // 2 * LANES, LANES)]
                code = word & 15 if b % 2 == 0 else word >> 4
                col = cols[pl.ds(b * LANES, LANES)].reshape(1, LANES) * (0.95 / 16.0)
                second[b, at_rows, :] = jnp.minimum(row, col) * (code.astype(jnp.float32) + 1.0)

    def decode_first():
        for load in loads[4:]:
            load.wait()
        wide = jnp.concatenate(
            [scales[...], jnp.zeros((LANES - BLOCKS, ROWS), jnp.float32)], axis=0
        )
        rowacc[...] = wide.T * (0.9 / 7.5)

        @pl.loop(0, ROWS // TILE)
        def _(i):
            at_rows = pl.ds(pl.multiple_of(i * TILE, TILE), TILE)
            scale = rowacc[at_rows, :]
            for b in range(BLOCKS):
                word = codes1[at_rows, pl.ds(b // 2 * LANES, LANES)]
                code = word & 15 if b % 2 == 0 else word >> 4
                mom[b, at_rows, :] = scale[:, b : b + 1] * (code.astype(jnp.float32) - 7.5)

    pl.semaphore_wait(barrier, len(partners))

    net = Copies(send, recv)
    ring = (1, 3, 2)

    def spread(n):
        for d in ring:
            other = (y + d) % NY
            net.start(
                ("b1", n, d),
                grads.at[:, pl.ds(other * PART + n * WIDTH, WIDTH)],
                bb.at[n, pl.ds(y * TOK, TOK)],
                to_y(d),
            )

    def pass_on(n, s, pieces=(0, 1, 2, 3)):
        for i in pieces:
            d = ((0,) + ring)[i]
            if s == 1 and d:
                net.arrived(("b1", n, d))
            elif s == 1:
                owns[n].wait()
            first = (y - d + NY) % NY * TOK
            for way in (1, -1):
                if s > 1:
                    net.arrived(("b2", n, s - 1, way, i))
                if s < 4 or (way > 0) == (i < 2):
                    net.start(
                        ("b2", n, s, way, i),
                        bb.at[n, pl.ds(place(way, s - 1) + first, TOK)],
                        bb.at[n, pl.ds(place(way, s) + first, TOK)],
                        to_z(way),
                    )

    pass_on(0, 1, (0,))
    spread(0)
    for d in ring:
        ref = spot(y, c, 0)
        net.start(("ay", 0, d), ref, ref, to_y(d))
        ref = spot(y, c, 1)
        net.start(("ax", 0, d), ref, ref, to_x(d))
    for d in ring:
        ref = spot(y, c, 0)
        net.start(("axy", 0, d), ref, ref, to_x(d))
        ref = spot(y, c, 1)
        net.start(("ayx", 0, d), ref, ref, to_y(d))
    pass_on(0, 1, (1, 2, 3))

    def relay(e):
        net.arrived(("ay", 0, e))
        ref = spot((y + NY - e) % NY, c, 0)
        for d in ring:
            net.start(("axy", e, d), ref, ref, to_x(d))
        net.arrived(("ax", 0, e))
        ref = spot(y, (x + NX - e) % NX * 2 + k, 1)
        for d in ring:
            net.start(("ayx", e, d), ref, ref, to_y(d))

    relay(1)
    pass_on(0, 2)
    relay(3)
    relay(2)
    spread(1)

    def to_peer(q):
        if q == 0:
            for d in ring:
                net.arrived(("ayx", 0, d))
        else:
            for e in (0,) + ring:
                net.arrived(("axy", e, q))
            for d in ring:
                net.arrived(("ayx", q, d))
        ref = at.at[:, tokens((x + NX - q) % NX * 2 + k)]
        net.start(("peer", q), ref, ref, peer)

    sq[...] = jnp.zeros_like(sq)

    order = (2, 1, 3, 0)

    def product(n, d, first, size):
        other = (y + d) % NY
        return jnp.dot(
            at[pl.ds(pl.multiple_of(other * ROWS, ROWS), ROWS), pl.ds(first, size)],
            bb[n, pl.ds(first, size)],
            preferred_element_type=jnp.float32,
        )

    def pack(n, d, res):
        tiles = res.reshape(ROWS // 8, 8, WIDTH)
        sq[...] += jnp.sum(tiles * tiles, axis=0)
        top = jnp.max(jnp.max(jnp.abs(tiles), axis=0), axis=0, keepdims=True)
        top = jnp.maximum(top, 1e-30)
        words = jnp.round(res * (32767.0 / top)).astype(jnp.int32).astype(jnp.int16)
        scale = jnp.broadcast_to(top * (1.0 / 32767.0), (8, WIDTH))
        block = y * (PART // LANES) + n * WB
        for w in range(WB):
            at_cols = slice(w * LANES, (w + 1) * LANES)
            if d:
                gs[n, d - 1, w] = words[:, at_cols]
                gs_scale[n, d - 1, w] = scale[:, at_cols]
            else:
                gi[block + w] = words[:, at_cols]
                gi_scale[block + w] = scale[:, at_cols]

    def hand_out(n, d):
        block = pl.ds(y * (PART // LANES) + n * WB, WB)
        net.start(("out", n, d), gs.at[n, d - 1], gi.at[block], to_y(d))
        net.start(("scale", n, d), gs_scale.at[n, d - 1], gi_scale.at[block], to_y(d))

    def far_arrived(n):
        for i in range(NY):
            net.arrived(("b2", n, 4, 1 if i < 2 else -1, i))

    decode_second()
    pass_on(0, 3)
    pass_on(1, 1)
    decode_first()
    pass_on(0, 4)
    pass_on(1, 2)
    for q in (0,) + ring:
        to_peer(q)
    pass_on(1, 3)
    for q in (0,) + ring:
        net.arrived(("peer", q))
    far_arrived(0)
    for d in order:
        pack(0, d, product(0, d, 0, TOKENS))
        if d:
            hand_out(0, d)
    pass_on(1, 4)
    for d in order:
        acc[d] = product(1, d, 0, FAR)
    far_arrived(1)
    for d in order:
        pack(1, d, acc[d] + product(1, d, FAR, ZROWS))

    ss_src[0] = jnp.full((8, LANES), jnp.sum(sq[...]))
    stages = [
        near,
        [(d, to_z(d)) for d in (4, 3, 5, 2, 6, 1, 7)],
        [(d, to_y(d)) for d in ring],
    ]
    slot = 0
    for i, stage in enumerate(stages):
        for j, (d, device) in enumerate(stage):
            net.start(("ss", i, d), ss_src.at[i], ss_dst.at[slot + j], device)
        if i == 0:
            for d in ring:
                hand_out(1, d)
        total = ss_src[i]
        for j, (d, device) in enumerate(stage):
            net.arrived(("ss", i, d))
            total = total + ss_dst[slot + j]
        slot += len(stage)
        if i < 2:
            ss_src[i + 1] = total
    limit = float(D) * FF
    clip = jnp.where(total <= limit, 1.0, jnp.sqrt(limit / jnp.maximum(total, limit)))

    for n in range(CHUNKS):
        for d in ring:
            net.arrived(("out", n, d))
            net.arrived(("scale", n, d))

    rate = clip[0:1, :]
    tenth = 0.1 * rate
    colacc[...] = jnp.zeros_like(colacc)

    @pl.loop(0, ROWS // TILE)
    def _(i):
        at_rows = pl.ds(pl.multiple_of(i * TILE, TILE), TILE)
        best = jnp.zeros((TILE, LANES), jnp.float32)
        for b in range(BLOCKS):
            words = gi[b, at_rows, :].astype(jnp.int32).astype(jnp.float32)
            scaled = words * (gi_scale[b, 0:1, :] * rate)
            value = second[b, at_rows, :] + 0.05 * scaled * scaled
            second[b, at_rows, :] = value
            best = jnp.maximum(best, value)
            colacc[b] = jnp.maximum(colacc[b], jnp.max(value.reshape(TILE // 8, 8, LANES), axis=0))
        rowacc[at_rows, :] = best

    for b in range(BLOCKS):
        cp_a[b : b + 1, :] = jnp.max(colacc[b], axis=0, keepdims=True)
    for j, d in enumerate(ring):
        net.start(("cy", d), cp_a, cp_dst.at[j], to_y(d))
    rp_a[...] = jnp.broadcast_to(jnp.max(rowacc[...].T, axis=0, keepdims=True), (8, ROWS))
    for j, (d, device) in enumerate(near):
        net.start(("rx", d), rp_a, rp_dst.at[j], device)

    def advance(first, last):
        lane = lax.broadcasted_iota(jnp.int32, (TILE, LANES), 1)

        @pl.loop(first, last)
        def _(i):
            at_rows = pl.ds(pl.multiple_of(i * TILE, TILE), TILE)
            peaks = jnp.zeros((TILE, LANES), jnp.float32)
            for b in range(BLOCKS):
                at_cols = pl.ds(b * LANES, LANES)
                words = gi[b, at_rows, :].astype(jnp.int32).astype(jnp.float32)
                value = mom[b, at_rows, :] + words * (gi_scale[b, 0:1, :] * tenth)
                peak = jnp.max(jnp.abs(value), axis=1, keepdims=True)
                peaks = jnp.where(lane == b, peak, peaks)
                first_normed[at_rows, at_cols] = (value * inverse(peak + 1e-06)).astype(
                    jnp.bfloat16
                )
                under = second[b, at_rows, :] * (1.0 / BIAS_TWO)
                root = under * lax.rsqrt(under) + 1e-08
                update[at_rows, at_cols] = (value * (1.0 / BIAS_ONE)) * inverse(root)
            rowacc[at_rows, :] = peaks

    advance(0, 3)
    for d in ring:
        net.arrived(("cy", d))
    cp_b[...] = jnp.maximum(
        jnp.maximum(cp_a[...], cp_dst[0]), jnp.maximum(cp_dst[1], cp_dst[2])
    )
    for d in (4, 3, 5, 2, 6, 1, 7):
        net.start(("cz", d), cp_b, cp_dst.at[2 + d], to_z(d))
    advance(3, ROWS // TILE)
    first_peaks[...] = rowacc[...].T[:BLOCKS, :]
    peaks = rp_a[...]
    for j, (d, _) in enumerate(near):
        net.arrived(("rx", d))
        peaks = jnp.maximum(peaks, rp_dst[j])
    rp_out[...] = peaks
    rinv_out[...] = jnp.broadcast_to((1.0 / peaks)[0:1, :], (LANES, ROWS)).T
    tops = cp_b[...]
    for d in range(1, NZ):
        net.arrived(("cz", d))
        tops = jnp.maximum(tops, cp_dst[2 + d])
    cp_out[...] = tops
    net.finish()


def inverse(value):
    guess = pltpu.reciprocal(value, approx=True)
    return guess * (2.0 - value * guess)


def finish_kernel(
    update_in,
    first_in,
    peaks_in,
    second,
    rinv,
    rp,
    cp,
    update,
    first_normed,
    first_peaks,
    second_normed,
    row_peaks,
    col_peaks,
    normed,
    sems,
):
    copies = [
        pltpu.make_async_copy(update_in, update, sems.at[0]),
        pltpu.make_async_copy(first_in, first_normed, sems.at[1]),
        pltpu.make_async_copy(peaks_in, first_peaks, sems.at[2]),
    ]
    for copy in copies:
        copy.start()
    row_peaks[...] = rp[0:1, :].reshape(ROWS)
    for b in range(BLOCKS):
        col_peaks[pl.ds(b * LANES, LANES)] = cp[b : b + 1, :].reshape(LANES)
    cinv = 1.0 / cp[...]
    for i in range(ROWS // FINISH):
        at_rows = pl.ds(i * FINISH, FINISH)
        for b in range(BLOCKS):
            normed[at_rows, pl.ds(b * LANES, LANES)] = (
                second[b, at_rows, :] * jnp.maximum(rinv[at_rows, :], cinv[b : b + 1, :])
            ).astype(jnp.bfloat16)
        copy = pltpu.make_async_copy(
            normed.at[at_rows], second_normed.at[at_rows], sems.at[3 + i]
        )
        copy.start()
        copies.append(copy)
    for copy in copies:
        copy.wait()


def local(activations, output_grads, first_codes, second_codes, first_scales, second_rows, second_cols):
    f32, bf16 = jnp.float32, jnp.bfloat16
    vmem = pl.BlockSpec(memory_space=pltpu.VMEM)
    hbm = pl.BlockSpec(memory_space=pltpu.HBM)
    update, first_normed, first_peaks, second, rinv, rp, cp = pl.pallas_call(
        step_kernel,
        out_shape=(
            jax.ShapeDtypeStruct((ROWS, COLS), f32),
            jax.ShapeDtypeStruct((ROWS, COLS), bf16),
            jax.ShapeDtypeStruct((BLOCKS, ROWS), f32),
            jax.ShapeDtypeStruct((BLOCKS, ROWS, LANES), f32),
            jax.ShapeDtypeStruct((ROWS, LANES), f32),
            jax.ShapeDtypeStruct((8, ROWS), f32),
            jax.ShapeDtypeStruct((BLOCKS, LANES), f32),
        ),
        in_specs=[hbm] * 7,
        out_specs=(vmem,) * 7,
        scratch_shapes=[
            pltpu.VMEM((ROWS, ROWS), bf16),
            pltpu.VMEM((ROWS, COLS // 2), jnp.int32),
            pltpu.VMEM((ROWS, COLS // 2), jnp.int32),
            pltpu.VMEM((BLOCKS, ROWS), f32),
            pltpu.VMEM((ROWS,), f32),
            pltpu.VMEM((COLS,), f32),
            pltpu.VMEM((NY * ROWS, TOKENS), bf16),
            pltpu.VMEM((CHUNKS, TOKENS, WIDTH), bf16),
            pltpu.VMEM((CHUNKS, 3, WB, ROWS, LANES), jnp.int16),
            pltpu.VMEM((CHUNKS, 3, WB, 8, LANES), f32),
            pltpu.VMEM((BLOCKS, ROWS, LANES), jnp.int16),
            pltpu.VMEM((BLOCKS, 8, LANES), f32),
            pltpu.VMEM((BLOCKS, ROWS, LANES), f32),
            pltpu.VMEM((NY, ROWS, WIDTH), f32),
            pltpu.VMEM((8, WIDTH), f32),
            pltpu.VMEM((3, 8, LANES), f32),
            pltpu.VMEM((17, 8, LANES), f32),
            pltpu.VMEM((BLOCKS, LANES), f32),
            pltpu.VMEM((BLOCKS, LANES), f32),
            pltpu.VMEM((10, BLOCKS, LANES), f32),
            pltpu.VMEM((8, ROWS), f32),
            pltpu.VMEM((7, 8, ROWS), f32),
            pltpu.VMEM((ROWS, LANES), f32),
            pltpu.VMEM((BLOCKS, 8, LANES), f32),
            pltpu.SemaphoreType.DMA((n_copies(),)),
            pltpu.SemaphoreType.DMA((n_copies(),)),
            pltpu.SemaphoreType.DMA((6 + CHUNKS,)),
        ],
        compiler_params=pltpu.CompilerParams(
            collective_id=0, has_side_effects=True, vmem_limit_bytes=40 * 2**20
        ),
        name="step",
    )(
        *(
            pltpu.with_memory_space_constraint(array, pltpu.HBM)
            for array in (
                activations,
                output_grads,
                first_codes,
                second_codes,
                first_scales.T,
                second_rows,
                second_cols,
            )
        )
    )
    update, first_normed, first_peaks, second_normed, row_peaks, col_peaks = pl.pallas_call(
        finish_kernel,
        out_shape=(
            jax.ShapeDtypeStruct((ROWS, COLS), f32),
            jax.ShapeDtypeStruct((ROWS, COLS), bf16),
            jax.ShapeDtypeStruct((BLOCKS, ROWS), f32),
            jax.ShapeDtypeStruct((ROWS, COLS), bf16),
            jax.ShapeDtypeStruct((ROWS,), f32),
            jax.ShapeDtypeStruct((COLS,), f32),
        ),
        in_specs=[vmem] * 7,
        out_specs=(hbm, hbm, hbm, hbm, vmem, vmem),
        scratch_shapes=[
            pltpu.VMEM((ROWS, COLS), bf16),
            pltpu.SemaphoreType.DMA((3 + ROWS // FINISH,)),
        ],
        compiler_params=pltpu.CompilerParams(vmem_limit_bytes=16 * 2**20),
        name="finish",
    )(update, first_normed, first_peaks, second, rinv, rp, cp)
    return update, first_normed, first_peaks.T, second_normed, row_peaks, col_peaks


def solution(mesh):
    return jax.shard_map(
        local,
        mesh=mesh,
        in_specs=(
            P("col", "row"),
            P("row", "col"),
            P("row", "col"),
            P("row", "col"),
            P("row", "col"),
            P("row"),
            P("col"),
        ),
        out_specs=(
            P("row", "col"),
            P("row", "col"),
            P("row", "col"),
            P("row", "col"),
            P("row"),
            P("col"),
        ),
        check_vma=False,
    )
```

```python
import jax
import jax.numpy as jnp
from jax import lax
from jax.experimental import pallas as pl
from jax.experimental.pallas import tpu as pltpu
from jax.sharding import PartitionSpec as P

MESH = pl.DeviceIdType.MESH
D = 8192
FF = 24576
TOKENS = 2048
ROWS = 256
COLS = 3072
NZ, NY, NX = 8, 4, 4
PART = COLS // NY
CHUNKS = 2
WIDTH = PART // CHUNKS
LANES = 128
WB = WIDTH // LANES
TILE = 32
FINISH = 64
BLOCKS = COLS // LANES
ZROWS = TOKENS // NZ
FAR = TOKENS - ZROWS
SPLIT = (192, 64)
TOK = TOKENS // (NZ * NY)

BIAS_ONE = 1.0 - 0.9**10
BIAS_TWO = 1.0 - 0.95**10


class Copies:
    def __init__(self, send, recv):
        self.send, self.recv = send, recv
        self.made = {}

    def start(self, key, src, dst, device):
        slot = len(self.made)
        copy = pltpu.make_async_remote_copy(
            src_ref=src,
            dst_ref=dst,
            send_sem=self.send.at[slot],
            recv_sem=self.recv.at[slot],
            device_id=device,
            device_id_type=MESH,
        )
        copy.start()
        self.made[key] = copy

    def arrived(self, key):
        self.made[key].wait_recv()

    def finish(self):
        for copy in self.made.values():
            copy.wait_send()


def n_copies():
    return CHUNKS * (3 + 28 + 3 + 3) + 6 + 24 + 4 + 17 + 10 + 7


def step_kernel(
    act_hbm,
    grads,
    codes1_hbm,
    codes2_hbm,
    scales_hbm,
    rows_hbm,
    cols_hbm,
    update,
    first_normed,
    first_peaks,
    second,
    rinv_out,
    rp_out,
    cp_out,
    act,
    codes1,
    codes2,
    scales,
    rows,
    cols,
    at,
    bb,
    gs,
    gs_scale,
    gi,
    gi_scale,
    mom,
    acc,
    sq,
    ss_src,
    ss_dst,
    cp_a,
    cp_b,
    cp_dst,
    rp_a,
    rp_dst,
    rowacc,
    colacc,
    send,
    recv,
    local,
):
    r, c = lax.axis_index("row"), lax.axis_index("col")
    z, y = r // NY, r % NY
    x, k = c // 2, c % 2

    def to_z(d):
        return ((z + d + NZ) % NZ * NY + y, c)

    def to_y(d):
        return (z * NY + (y + d) % NY, c)

    def to_x(d):
        return (r, (x + d) % NX * 2 + k)

    peer = (r, x * 2 + 1 - k)
    near = [(d, to_x(d)) for d in (1, 3, 2)] + [
        (4 + d, (r, (x + d) % NX * 2 + 1 - k)) for d in (0, 1, 3, 2)
    ]

    barrier = pltpu.get_barrier_semaphore()
    partners = (
        [to_z(d) for d in (1, 7)]
        + [to_y(d) for d in (1, 3, 2)]
        + [device for d, device in near if d <= 4]
    )
    for partner in partners:
        pl.semaphore_signal(barrier, inc=1, device_id=partner, device_id_type=MESH)

    pairs = (
        (act_hbm, act),
        (codes2_hbm, codes2),
        (rows_hbm, rows),
        (cols_hbm, cols),
        (scales_hbm, scales),
        (codes1_hbm, codes1),
    )
    loads = [pltpu.make_async_copy(src, dst, local.at[i]) for i, (src, dst) in enumerate(pairs)]
    for load in loads:
        load.start()

    def place(way, distance):
        if distance == 4:
            return FAR
        return (distance if way < 0 or distance == 0 else 3 + distance) * ZROWS

    def tokens(cc):
        ahead = (cc - z + NZ) % NZ
        return pl.ds((ahead + ahead // 4 * (11 - 2 * ahead)) * ROWS, ROWS)

    def spot(yy, cc, half=None):
        if half is None:
            return at.at[pl.ds(yy * ROWS, ROWS), tokens(cc)]
        return at.at[pl.ds(yy * ROWS + half * SPLIT[0], SPLIT[half]), tokens(cc)]

    owns = []
    for n in range(CHUNKS):
        own = pltpu.make_async_copy(
            grads.at[:, pl.ds(y * PART + n * WIDTH, WIDTH)],
            bb.at[n, pl.ds(y * TOK, TOK)],
            local.at[len(pairs) + n],
        )
        own.start()
        owns.append(own)

    def decode_second():
        for load in loads[1:4]:
            load.wait()
        rowacc[...] = jnp.broadcast_to(rows[...].reshape(1, ROWS), (LANES, ROWS)).T * (0.95 / 16.0)

        @pl.loop(0, ROWS // TILE)
        def _(i):
            at_rows = pl.ds(pl.multiple_of(i * TILE, TILE), TILE)
            row = rowacc[at_rows, :]
            for b in range(BLOCKS):
                word = codes2[at_rows, pl.ds(b // 2 * LANES, LANES)]
                code = word & 15 if b % 2 == 0 else word >> 4
                col = cols[pl.ds(b * LANES, LANES)].reshape(1, LANES) * (0.95 / 16.0)
                second[b, at_rows, :] = jnp.minimum(row, col) * (code.astype(jnp.float32) + 1.0)

    def decode_first():
        for load in loads[4:]:
            load.wait()
        wide = jnp.concatenate(
            [scales[...], jnp.zeros((LANES - BLOCKS, ROWS), jnp.float32)], axis=0
        )
        rowacc[...] = wide.T * (0.9 / 7.5)

        @pl.loop(0, ROWS // TILE)
        def _(i):
            at_rows = pl.ds(pl.multiple_of(i * TILE, TILE), TILE)
            scale = rowacc[at_rows, :]
            for b in range(BLOCKS):
                word = codes1[at_rows, pl.ds(b // 2 * LANES, LANES)]
                code = word & 15 if b % 2 == 0 else word >> 4
                mom[b, at_rows, :] = scale[:, b : b + 1] * (code.astype(jnp.float32) - 7.5)

    pl.semaphore_wait(barrier, len(partners))

    net = Copies(send, recv)
    ring = (1, 3, 2)

    def spread(n):
        for d in ring:
            other = (y + d) % NY
            net.start(
                ("b1", n, d),
                grads.at[:, pl.ds(other * PART + n * WIDTH, WIDTH)],
                bb.at[n, pl.ds(y * TOK, TOK)],
                to_y(d),
            )

    def pass_on(n, s, pieces=(0, 1, 2, 3)):
        for i in pieces:
            d = ((0,) + ring)[i]
            if s == 1 and d:
                net.arrived(("b1", n, d))
            elif s == 1:
                owns[n].wait()
            first = (y - d + NY) % NY * TOK
            for way in (1, -1):
                if s > 1:
                    net.arrived(("b2", n, s - 1, way, i))
                if s < 4 or (way > 0) == (i < 2):
                    net.start(
                        ("b2", n, s, way, i),
                        bb.at[n, pl.ds(place(way, s - 1) + first, TOK)],
                        bb.at[n, pl.ds(place(way, s) + first, TOK)],
                        to_z(way),
                    )

    pass_on(0, 1, (0,))
    spread(0)
    loads[0].wait()
    spot(y, c)[...] = act[...].T
    for d in ring:
        ref = spot(y, c, 0)
        net.start(("ay", 0, d), ref, ref, to_y(d))
        ref = spot(y, c, 1)
        net.start(("ax", 0, d), ref, ref, to_x(d))
    for d in ring:
        ref = spot(y, c, 0)
        net.start(("axy", 0, d), ref, ref, to_x(d))
        ref = spot(y, c, 1)
        net.start(("ayx", 0, d), ref, ref, to_y(d))
    pass_on(0, 1, (1, 2, 3))

    def relay(e):
        net.arrived(("ay", 0, e))
        ref = spot((y + NY - e) % NY, c, 0)
        for d in ring:
            net.start(("axy", e, d), ref, ref, to_x(d))
        net.arrived(("ax", 0, e))
        ref = spot(y, (x + NX - e) % NX * 2 + k, 1)
        for d in ring:
            net.start(("ayx", e, d), ref, ref, to_y(d))

    relay(1)
    pass_on(0, 2)
    relay(3)
    relay(2)
    spread(1)

    def to_peer(q):
        if q == 0:
            for d in ring:
                net.arrived(("ayx", 0, d))
        else:
            for e in (0,) + ring:
                net.arrived(("axy", e, q))
            for d in ring:
                net.arrived(("ayx", q, d))
        ref = at.at[:, tokens((x + NX - q) % NX * 2 + k)]
        net.start(("peer", q), ref, ref, peer)

    sq[...] = jnp.zeros_like(sq)

    order = (2, 1, 3, 0)

    def product(n, d, first, size):
        other = (y + d) % NY
        return jnp.dot(
            at[pl.ds(pl.multiple_of(other * ROWS, ROWS), ROWS), pl.ds(first, size)],
            bb[n, pl.ds(first, size)],
            preferred_element_type=jnp.float32,
        )

    def pack(n, d, res):
        tiles = res.reshape(ROWS // 8, 8, WIDTH)
        sq[...] += jnp.sum(tiles * tiles, axis=0)
        top = jnp.max(jnp.max(jnp.abs(tiles), axis=0), axis=0, keepdims=True)
        top = jnp.maximum(top, 1e-30)
        words = jnp.round(res * (32767.0 / top)).astype(jnp.int32).astype(jnp.int16)
        scale = jnp.broadcast_to(top * (1.0 / 32767.0), (8, WIDTH))
        block = y * (PART // LANES) + n * WB
        for w in range(WB):
            at_cols = slice(w * LANES, (w + 1) * LANES)
            if d:
                gs[n, d - 1, w] = words[:, at_cols]
                gs_scale[n, d - 1, w] = scale[:, at_cols]
            else:
                gi[block + w] = words[:, at_cols]
                gi_scale[block + w] = scale[:, at_cols]

    def hand_out(n, d):
        block = pl.ds(y * (PART // LANES) + n * WB, WB)
        net.start(("out", n, d), gs.at[n, d - 1], gi.at[block], to_y(d))
        net.start(("scale", n, d), gs_scale.at[n, d - 1], gi_scale.at[block], to_y(d))

    def far_arrived(n):
        for i in range(NY):
            net.arrived(("b2", n, 4, 1 if i < 2 else -1, i))

    decode_second()
    pass_on(0, 3)
    pass_on(1, 1)
    decode_first()
    pass_on(0, 4)
    pass_on(1, 2)
    for q in (0,) + ring:
        to_peer(q)
    pass_on(1, 3)
    for q in (0,) + ring:
        net.arrived(("peer", q))
    far_arrived(0)
    for d in order:
        pack(0, d, product(0, d, 0, TOKENS))
        if d:
            hand_out(0, d)
    pass_on(1, 4)
    for d in order:
        acc[d] = product(1, d, 0, FAR)
    far_arrived(1)
    for d in order:
        pack(1, d, acc[d] + product(1, d, FAR, ZROWS))

    ss_src[0] = jnp.full((8, LANES), jnp.sum(sq[...]))
    stages = [
        near,
        [(d, to_z(d)) for d in (4, 3, 5, 2, 6, 1, 7)],
        [(d, to_y(d)) for d in ring],
    ]
    slot = 0
    for i, stage in enumerate(stages):
        for j, (d, device) in enumerate(stage):
            net.start(("ss", i, d), ss_src.at[i], ss_dst.at[slot + j], device)
        if i == 0:
            for d in ring:
                hand_out(1, d)
        total = ss_src[i]
        for j, (d, device) in enumerate(stage):
            net.arrived(("ss", i, d))
            total = total + ss_dst[slot + j]
        slot += len(stage)
        if i < 2:
            ss_src[i + 1] = total
    limit = float(D) * FF
    clip = jnp.where(total <= limit, 1.0, jnp.sqrt(limit / jnp.maximum(total, limit)))

    for n in range(CHUNKS):
        for d in ring:
            net.arrived(("out", n, d))
            net.arrived(("scale", n, d))

    rate = clip[0:1, :]
    tenth = 0.1 * rate
    colacc[...] = jnp.zeros_like(colacc)

    @pl.loop(0, ROWS // TILE)
    def _(i):
        at_rows = pl.ds(pl.multiple_of(i * TILE, TILE), TILE)
        best = jnp.zeros((TILE, LANES), jnp.float32)
        for b in range(BLOCKS):
            words = gi[b, at_rows, :].astype(jnp.int32).astype(jnp.float32)
            scaled = words * (gi_scale[b, 0:1, :] * rate)
            value = second[b, at_rows, :] + 0.05 * scaled * scaled
            second[b, at_rows, :] = value
            best = jnp.maximum(best, value)
            colacc[b] = jnp.maximum(colacc[b], jnp.max(value.reshape(TILE // 8, 8, LANES), axis=0))
        rowacc[at_rows, :] = best

    for b in range(BLOCKS):
        cp_a[b : b + 1, :] = jnp.max(colacc[b], axis=0, keepdims=True)
    for j, d in enumerate(ring):
        net.start(("cy", d), cp_a, cp_dst.at[j], to_y(d))
    rp_a[...] = jnp.broadcast_to(jnp.max(rowacc[...].T, axis=0, keepdims=True), (8, ROWS))
    for j, (d, device) in enumerate(near):
        net.start(("rx", d), rp_a, rp_dst.at[j], device)

    def advance(first, last):
        lane = lax.broadcasted_iota(jnp.int32, (TILE, LANES), 1)

        @pl.loop(first, last)
        def _(i):
            at_rows = pl.ds(pl.multiple_of(i * TILE, TILE), TILE)
            peaks = jnp.zeros((TILE, LANES), jnp.float32)
            for b in range(BLOCKS):
                at_cols = pl.ds(b * LANES, LANES)
                words = gi[b, at_rows, :].astype(jnp.int32).astype(jnp.float32)
                value = mom[b, at_rows, :] + words * (gi_scale[b, 0:1, :] * tenth)
                peak = jnp.max(jnp.abs(value), axis=1, keepdims=True)
                peaks = jnp.where(lane == b, peak, peaks)
                first_normed[at_rows, at_cols] = (value * inverse(peak + 1e-06)).astype(
                    jnp.bfloat16
                )
                under = second[b, at_rows, :] * (1.0 / BIAS_TWO)
                root = under * lax.rsqrt(under) + 1e-08
                update[at_rows, at_cols] = (value * (1.0 / BIAS_ONE)) * inverse(root)
            rowacc[at_rows, :] = peaks

    advance(0, 3)
    for d in ring:
        net.arrived(("cy", d))
    cp_b[...] = jnp.maximum(
        jnp.maximum(cp_a[...], cp_dst[0]), jnp.maximum(cp_dst[1], cp_dst[2])
    )
    for d in (4, 3, 5, 2, 6, 1, 7):
        net.start(("cz", d), cp_b, cp_dst.at[2 + d], to_z(d))
    advance(3, ROWS // TILE)
    first_peaks[...] = rowacc[...].T[:BLOCKS, :]
    peaks = rp_a[...]
    for j, (d, _) in enumerate(near):
        net.arrived(("rx", d))
        peaks = jnp.maximum(peaks, rp_dst[j])
    rp_out[...] = peaks
    rinv_out[...] = jnp.broadcast_to((1.0 / peaks)[0:1, :], (LANES, ROWS)).T
    tops = cp_b[...]
    for d in range(1, NZ):
        net.arrived(("cz", d))
        tops = jnp.maximum(tops, cp_dst[2 + d])
    cp_out[...] = tops
    net.finish()


def inverse(value):
    guess = pltpu.reciprocal(value, approx=True)
    return guess * (2.0 - value * guess)


def finish_kernel(
    update_in,
    first_in,
    peaks_in,
    second,
    rinv,
    rp,
    cp,
    update,
    first_normed,
    first_peaks,
    second_normed,
    row_peaks,
    col_peaks,
    normed,
    row_line,
    col_line,
    sems,
):
    copies = [
        pltpu.make_async_copy(update_in, update, sems.at[0]),
        pltpu.make_async_copy(first_in, first_normed, sems.at[1]),
        pltpu.make_async_copy(peaks_in, first_peaks, sems.at[2]),
    ]
    for copy in copies:
        copy.start()
    row_line[...] = rp[0:1, :].reshape(ROWS)
    for b in range(BLOCKS):
        col_line[pl.ds(b * LANES, LANES)] = cp[b : b + 1, :].reshape(LANES)
    lines = [
        pltpu.make_async_copy(row_line, row_peaks, sems.at[3 + ROWS // FINISH]),
        pltpu.make_async_copy(col_line, col_peaks, sems.at[4 + ROWS // FINISH]),
    ]
    for line in lines:
        line.start()
    copies += lines
    cinv = 1.0 / cp[...]
    for i in range(ROWS // FINISH):
        at_rows = pl.ds(i * FINISH, FINISH)
        for b in range(BLOCKS):
            normed[at_rows, pl.ds(b * LANES, LANES)] = (
                second[b, at_rows, :] * jnp.maximum(rinv[at_rows, :], cinv[b : b + 1, :])
            ).astype(jnp.bfloat16)
        copy = pltpu.make_async_copy(
            normed.at[at_rows], second_normed.at[at_rows], sems.at[3 + i]
        )
        copy.start()
        copies.append(copy)
    for copy in copies:
        copy.wait()


def local(activations, output_grads, first_codes, second_codes, first_scales, second_rows, second_cols):
    f32, bf16 = jnp.float32, jnp.bfloat16
    vmem = pl.BlockSpec(memory_space=pltpu.VMEM)
    hbm = pl.BlockSpec(memory_space=pltpu.HBM)
    update, first_normed, first_peaks, second, rinv, rp, cp = pl.pallas_call(
        step_kernel,
        out_shape=(
            jax.ShapeDtypeStruct((ROWS, COLS), f32),
            jax.ShapeDtypeStruct((ROWS, COLS), bf16),
            jax.ShapeDtypeStruct((BLOCKS, ROWS), f32),
            jax.ShapeDtypeStruct((BLOCKS, ROWS, LANES), f32),
            jax.ShapeDtypeStruct((ROWS, LANES), f32),
            jax.ShapeDtypeStruct((8, ROWS), f32),
            jax.ShapeDtypeStruct((BLOCKS, LANES), f32),
        ),
        in_specs=[hbm] * 7,
        out_specs=(vmem,) * 7,
        scratch_shapes=[
            pltpu.VMEM((ROWS, ROWS), bf16),
            pltpu.VMEM((ROWS, COLS // 2), jnp.int32),
            pltpu.VMEM((ROWS, COLS // 2), jnp.int32),
            pltpu.VMEM((BLOCKS, ROWS), f32),
            pltpu.VMEM((ROWS,), f32),
            pltpu.VMEM((COLS,), f32),
            pltpu.VMEM((NY * ROWS, TOKENS), bf16),
            pltpu.VMEM((CHUNKS, TOKENS, WIDTH), bf16),
            pltpu.VMEM((CHUNKS, 3, WB, ROWS, LANES), jnp.int16),
            pltpu.VMEM((CHUNKS, 3, WB, 8, LANES), f32),
            pltpu.VMEM((BLOCKS, ROWS, LANES), jnp.int16),
            pltpu.VMEM((BLOCKS, 8, LANES), f32),
            pltpu.VMEM((BLOCKS, ROWS, LANES), f32),
            pltpu.VMEM((NY, ROWS, WIDTH), f32),
            pltpu.VMEM((8, WIDTH), f32),
            pltpu.VMEM((3, 8, LANES), f32),
            pltpu.VMEM((17, 8, LANES), f32),
            pltpu.VMEM((BLOCKS, LANES), f32),
            pltpu.VMEM((BLOCKS, LANES), f32),
            pltpu.VMEM((10, BLOCKS, LANES), f32),
            pltpu.VMEM((8, ROWS), f32),
            pltpu.VMEM((7, 8, ROWS), f32),
            pltpu.VMEM((ROWS, LANES), f32),
            pltpu.VMEM((BLOCKS, 8, LANES), f32),
            pltpu.SemaphoreType.DMA((n_copies(),)),
            pltpu.SemaphoreType.DMA((n_copies(),)),
            pltpu.SemaphoreType.DMA((6 + CHUNKS,)),
        ],
        compiler_params=pltpu.CompilerParams(
            collective_id=0, has_side_effects=True, vmem_limit_bytes=40 * 2**20
        ),
        name="step",
    )(
        *(
            pltpu.with_memory_space_constraint(array, pltpu.HBM)
            for array in (
                activations,
                output_grads,
                first_codes,
                second_codes,
                first_scales.T,
                second_rows,
                second_cols,
            )
        )
    )
    update, first_normed, first_peaks, second_normed, row_peaks, col_peaks = pl.pallas_call(
        finish_kernel,
        out_shape=(
            jax.ShapeDtypeStruct((ROWS, COLS), f32),
            jax.ShapeDtypeStruct((ROWS, COLS), bf16),
            jax.ShapeDtypeStruct((BLOCKS, ROWS), f32),
            jax.ShapeDtypeStruct((ROWS, COLS), bf16),
            jax.ShapeDtypeStruct((ROWS,), f32),
            jax.ShapeDtypeStruct((COLS,), f32),
        ),
        in_specs=[vmem] * 7,
        out_specs=(hbm,) * 6,
        scratch_shapes=[
            pltpu.VMEM((ROWS, COLS), bf16),
            pltpu.VMEM((ROWS,), f32),
            pltpu.VMEM((COLS,), f32),
            pltpu.SemaphoreType.DMA((5 + ROWS // FINISH,)),
        ],
        compiler_params=pltpu.CompilerParams(vmem_limit_bytes=16 * 2**20),
        name="finish",
    )(update, first_normed, first_peaks, second, rinv, rp, cp)
    return update, first_normed, first_peaks.T, second_normed, row_peaks, col_peaks


def solution(mesh):
    return jax.shard_map(
        local,
        mesh=mesh,
        in_specs=(
            P("col", "row"),
            P("row", "col"),
            P("row", "col"),
            P("row", "col"),
            P("row", "col"),
            P("row"),
            P("col"),
        ),
        out_specs=(
            P("row", "col"),
            P("row", "col"),
            P("row", "col"),
            P("row", "col"),
            P("row"),
            P("col"),
        ),
        check_vma=False,
    )
```
